1024 devices in a mesh: dp: 4 (over y_lo), ctx: 32 (over y_hi, z), tp: 8 (over x, core).
Axes of the slice: x: 4, y: 8 (y_hi: 2, y_lo: 4; y = y_hi * 4 + y_lo), z: 16, core: 2. Of those that a mesh axis runs over, the one named last changes fastest.
Arguments:
- layer_input: bfloat16 [4, 4096, 8192], P('dp', 'ctx'), may hold values from -6 to 6
- queries: bfloat16 [4, 4096, 16384], P('dp', 'ctx', 'tp'), may hold values from -6 to 6
- key_heads: bfloat16 [4, 4096, 1024], P('dp', 'ctx', 'tp'), may hold values from -6 to 6
- value_heads: bfloat16 [4, 4096, 1024], P('dp', 'ctx', 'tp'), may hold values from -6 to 6
- attn_out: bfloat16 [4, 4096, 16384], P('dp', 'ctx', 'tp'), may hold values from -6 to 6
- out_grad: bfloat16 [4, 4096, 16384], P('dp', 'ctx', 'tp'), may hold values from -6 to 6
- log_sums: float32 [4, 128, 4096], P('dp', 'tp', 'ctx'), may hold values from 4 to 7
- doc_ids: int32 [4, 4096], P('dp'), may hold values from 0 to 63, never falling along the last dimension, each value on 1 to 193 neighbouring positions
Outputs:
- query_grad: bfloat16 [4, 4096, 16384], P('dp', 'ctx', 'tp')
- key_grad: bfloat16 [4, 4096, 1024], P('dp', 'ctx', 'tp')
- value_grad: bfloat16 [4, 4096, 1024], P('dp', 'ctx', 'tp')
- weight_grad: float32 [8192, 1024], P(('dp', 'ctx'), 'tp')
The draws below stay inside these ranges and needn't reach their ends.
Inputs may be any that keep to these rules, and one draw needn't show every extreme that they name: `doc_ids`: along each sequence's positions the document ids never fall; every id names 1 to 193 positions, and one names exactly 193.
All inputs are finite; a program needn't handle non-finite values.
Results may differ from the reference program's by a relative error of at most 0.0061.
Values may be sent and summed in bfloat16 or wider, within the bound.
No kernel may reach another device: no remote copies, remote signals or barrier semaphores. Data moves between devices by JAX's collectives and lax.ppermute only.
A program may use at most 64 MiB of HBM per device.

```python
import math
import jax
import jax.numpy as jnp
import numpy as np
from jax import lax

C = 64
REACH = 4
HQ = 128
KVH = 8
HD = 128
D = 8192
BATCH = 4
SEQ = 4096
MAXDOC = 193
DOCS = 64
N_CTX = 32


def strengthened(entries, key, source, target, shards_of, factor):
    def block_of(position):
        return (jnp.arange(entries.shape[position]) // (entries.shape[position] // shards_of)).reshape((-1,) + (1,) * (entries.ndim - 1 - position))

    near = jax.random.permutation(key, shards_of)[block_of(target)]
    far = (block_of(target) + shards_of // 2) % shards_of
    return jnp.where((block_of(source) == near) | (block_of(source) == far), factor * entries, entries)


def block_scale(own_key, shape, split, low, top_value):
    loudness = 1.0
    for position, parts in split:
        steps = jax.random.uniform(jax.random.fold_in(jax.random.fold_in(own_key, 6), position), (parts,), jnp.float32, low / len(split), top_value / len(split))
        loudness = loudness * jnp.repeat(jnp.exp(steps), shape[position] // parts).reshape((-1,) + (1,) * (len(shape) - 1 - position))
    return loudness


def split_up(number_of, total, most, slope):
    loads = [(1 << 20) // math.isqrt(standing ** slope) + 1 for standing in range(2, number_of + 1)]
    rest, holding = total - most - (number_of - 1), [1] * (number_of - 1)
    while rest > 0:
        movable = [i for i in range(number_of - 1) if holding[i] < most]
        pool, left = sum([loads[i] for i in movable]), rest
        for i in movable:
            extra = min(most - holding[i], max(1, left * loads[i] // pool), rest)
            holding[i] = holding[i] + extra
            rest = rest - extra
    return np.array([most] + holding)


def ragged_sizes(stream_key, count, total, most, skew):
    if count == 2:
        one = jax.random.randint(stream_key, (), max(1, total - most), min(most, total - 1) + 1)
        return jnp.stack([one, total - one])
    lengths = jnp.asarray(split_up(count, total, most, skew), jnp.int32)
    twos = (count - 1) // 2
    giver, sink = lengths[1:1 + 2 * twos:2], lengths[2:2 + 2 * twos:2]
    room = jnp.minimum(giver - 1, most - sink)
    passed = jax.random.randint(jax.random.fold_in(stream_key, 1), (twos,), 0, 1 << 20) % (room + 1)
    lengths = lengths.at[1:1 + 2 * twos:2].set(giver - passed).at[2:2 + 2 * twos:2].set(sink + passed)
    return lengths[jax.random.permutation(jax.random.fold_in(stream_key, 2), count)]


def centred(rng, dims, spread, bound, split=(), held_as=jnp.bfloat16):
    array = spread * jax.random.normal(rng, dims, jnp.float32)
    if split:
        array = array * block_scale(rng, dims, split, -0.22, 0.18)
    return jnp.clip(array, -bound, bound).astype(held_as)


def gaussian_with(own_key, shape, deviation, bound, split, heavy, held_as=jnp.bfloat16):
    drawn = deviation * jax.random.normal(own_key, shape, jnp.float32)
    if split:
        drawn = drawn * block_scale(own_key, shape, split, -0.22, 0.18)
    return jnp.clip(strengthened(drawn, jax.random.fold_in(own_key, 3), *heavy), -bound, bound).astype(held_as)


def setup_inputs(seed: int = 0) -> dict:
    key_of = jax.random.split(jax.random.key(seed), 9)
    return {
        "layer_input": gaussian_with(key_of[0], (BATCH, SEQ, D), 1.0, 6.0, ((0, 4), (1, 32)), (1, 2, 32, 2.75)),
        "queries": centred(key_of[1], (BATCH, SEQ, HQ * HD), 1.0, 6.0, ((0, 4), (1, 32), (2, 8))),
        "key_heads": centred(key_of[2], (BATCH, SEQ, KVH * HD), 1.0, 6.0, ((0, 4), (1, 32), (2, 8))),
        "value_heads": centred(key_of[3], (BATCH, SEQ, KVH * HD), 1.0, 6.0, ((0, 4), (1, 32), (2, 8))),
        "attn_out": centred(key_of[4], (BATCH, SEQ, HQ * HD), 1.0, 6.0, ((0, 4), (1, 32), (2, 8))),
        "out_grad": centred(key_of[5], (BATCH, SEQ, HQ * HD), 1.0, 6.0, ((0, 4), (1, 32), (2, 8))),
        "log_sums": jnp.clip(4.0 + 3.0 * jax.random.uniform(key_of[6], (BATCH, HQ, SEQ), jnp.float32) ** block_scale(key_of[6], (BATCH, HQ, SEQ), ((0, 4), (1, 8), (2, 32)), -0.2, 0.2), 4.0, 7.0),
        "doc_ids": jax.vmap(lambda own: jnp.searchsorted(jnp.cumsum(ragged_sizes(own, DOCS, SEQ, MAXDOC, 1)), jnp.arange(SEQ), side="right"))(jax.random.split(key_of[7], BATCH)).reshape((BATCH, SEQ)).astype(jnp.int32),
    }


def seq_order(stored):
    blocks = stored.reshape(N_CTX, 2, C, stored.shape[-1])
    return jnp.concatenate([blocks[:, 0], blocks[::-1, 1]], axis=0)


def store_order(ordered):
    lower = ordered[:N_CTX]
    upper = ordered[N_CTX:][::-1]
    return jnp.stack([lower, upper], axis=1).reshape(SEQ, ordered.shape[-1])


def one_sequence(queries, key_heads, value_heads, attn_out, out_grad, log_sums, doc_seq):
    per_group = HQ // KVH
    score_scale = HD ** -0.5
    margin = (REACH - 1) * C
    key_span = REACH * C
    query_blocks = seq_order(queries).reshape(2 * N_CTX, C, KVH, per_group, HD)
    grad_blocks = seq_order(out_grad).reshape(2 * N_CTX, C, KVH, per_group, HD)
    out_blocks = seq_order(attn_out).reshape(2 * N_CTX, C, KVH, per_group, HD)
    lse_blocks = seq_order(log_sums.T).reshape(2 * N_CTX, C, KVH, per_group)
    pad_rows = jnp.zeros((margin, KVH * HD), jnp.bfloat16)
    key_seq = jnp.concatenate([pad_rows, seq_order(key_heads).reshape(SEQ, KVH * HD)], axis=0)
    value_seq = jnp.concatenate([pad_rows, seq_order(value_heads).reshape(SEQ, KVH * HD)], axis=0)
    doc_int = doc_seq.astype(jnp.int32)
    doc_pad = jnp.concatenate([jnp.full((margin,), -1, jnp.int32), doc_int], axis=0)
    offsets = jnp.arange(C, dtype=jnp.int32)
    key_offsets = jnp.arange(key_span, dtype=jnp.int32)

    def visit_block(running, inputs):
        grad_keys, grad_values = running
        block_index, query_rows, grad_rows, out_rows, lse_block = inputs
        start_row = block_index * C
        query_full = query_rows.astype(jnp.float32)
        grad_full = grad_rows.astype(jnp.float32)
        out_full = out_rows.astype(jnp.float32)
        key_full = lax.dynamic_slice_in_dim(key_seq, start_row, key_span, 0).astype(jnp.float32).reshape(key_span, KVH, HD)
        value_full = lax.dynamic_slice_in_dim(value_seq, start_row, key_span, 0).astype(jnp.float32).reshape(key_span, KVH, HD)
        key_doc = lax.dynamic_slice_in_dim(doc_pad, start_row, key_span, 0)
        query_doc = lax.dynamic_slice_in_dim(doc_int, start_row, C, 0)
        query_pos = start_row + offsets
        key_pos = start_row - margin + key_offsets
        live_mask = (key_pos[None, :] <= query_pos[:, None]) & (key_doc[None, :] == query_doc[:, None])
        lse_rows = lse_block.transpose(1, 2, 0)
        scores = jnp.einsum("qgrd,kgd->grqk", query_full, key_full) * score_scale
        soft_probs = jnp.where(live_mask, jnp.exp(scores - lse_rows[..., None]), 0.0)
        probs_bf = lax.optimization_barrier(soft_probs.astype(jnp.bfloat16)).astype(jnp.float32)
        grad_value = jnp.einsum("grqk,qgrd->kgd", probs_bf, grad_full)
        grad_probs = jnp.einsum("qgrd,kgd->grqk", grad_full, value_full)
        row_delta = jnp.sum(grad_full * out_full, axis=-1).transpose(1, 2, 0)
        grad_scores = lax.optimization_barrier((soft_probs * (grad_probs - row_delta[..., None])).astype(jnp.bfloat16)).astype(jnp.float32)
        grad_query = jnp.einsum("grqk,kgd->qgrd", grad_scores, key_full) * score_scale
        grad_key = jnp.einsum("grqk,qgrd->kgd", grad_scores, query_full) * score_scale
        grad_keys = lax.dynamic_update_slice_in_dim(grad_keys, lax.dynamic_slice_in_dim(grad_keys, start_row, key_span, 0) + grad_key.reshape(key_span, KVH * HD), start_row, 0)
        grad_values = lax.dynamic_update_slice_in_dim(grad_values, lax.dynamic_slice_in_dim(grad_values, start_row, key_span, 0) + grad_value.reshape(key_span, KVH * HD), start_row, 0)
        return (grad_keys, grad_values), grad_query.reshape(C, HQ * HD)

    zeros_rows = jnp.zeros((SEQ + margin, KVH * HD), jnp.float32)
    blocks = jnp.arange(2 * N_CTX, dtype=jnp.int32)
    (grad_keys, grad_values), grad_queries = lax.scan(visit_block, (zeros_rows, zeros_rows), (blocks, query_blocks, grad_blocks, out_blocks, lse_blocks))
    grad_keys = store_order(grad_keys[margin:].reshape(2 * N_CTX, C, KVH * HD))
    grad_values = store_order(grad_values[margin:].reshape(2 * N_CTX, C, KVH * HD))
    grad_queries = store_order(grad_queries)
    return grad_queries.astype(jnp.bfloat16), grad_keys.astype(jnp.bfloat16), grad_values.astype(jnp.bfloat16)


def reference(layer_input, queries, key_heads, value_heads, attn_out, out_grad, log_sums, doc_ids):
    query_list = []
    key_list = []
    value_list = []
    for batch_row in range(queries.shape[0]):
        results = one_sequence(queries[batch_row], key_heads[batch_row], value_heads[batch_row], attn_out[batch_row], out_grad[batch_row], log_sums[batch_row], doc_ids[batch_row])
        query_list.append(results[0])
        key_list.append(results[1])
        value_list.append(results[2])
    query_grad = jnp.stack(query_list, axis=0)
    key_grad = jnp.stack(key_list, axis=0)
    value_grad = jnp.stack(value_list, axis=0)
    total = jnp.zeros((layer_input.shape[2], KVH * HD), jnp.float32)
    for batch_row in range(queries.shape[0]):
        total = total + jnp.dot(layer_input[batch_row].T, value_grad[batch_row], preferred_element_type=jnp.float32)
    weight_grad = total * (queries.shape[0] * SEQ) ** -0.5
    return query_grad, key_grad, value_grad, weight_grad
```

```python
import functools

import jax
import jax.numpy as jnp
from jax import lax
from jax.experimental import pallas as pl
from jax.experimental.pallas import tpu as pltpu
from jax.sharding import Mesh
from jax.sharding import PartitionSpec as P

HD = 128
C = 64
CTX = ("ctx_0", "ctx_1")
ROWS = ("dp", "ctx_0")
DP_CTX = ("dp", "ctx_0", "ctx_1")
SCALE = HD ** (-0.5)
BF = jnp.bfloat16
F32 = jnp.float32
SMEM = pl.BlockSpec(memory_space=pltpu.SMEM)
VMEM = pl.BlockSpec(memory_space=pltpu.VMEM)


def call(kernel, outs, n_in, flops, scratch=()):
    return pl.pallas_call(
        kernel,
        out_shape=outs,
        in_specs=[SMEM] + [VMEM] * (n_in - 1),
        out_specs=[VMEM] * len(outs),
        scratch_shapes=list(scratch),
        compiler_params=pltpu.CompilerParams(vmem_limit_bytes=40 * 1024 * 1024),
        cost_estimate=pl.CostEstimate(flops=flops, bytes_accessed=1 << 20, transcendentals=0),
    )


def shape(dims, dtype):
    return jax.ShapeDtypeStruct(dims, dtype)


def doc_pair(doc_ref, block):
    first = jnp.maximum(block - 1, 0)
    chunk = first // 2
    ahead = jnp.minimum(chunk + 1, doc_ref.shape[1] // 128 - 1)
    here = doc_ref[:, pl.ds(pl.multiple_of(chunk * 128, 128), 128)]
    after = doc_ref[:, pl.ds(pl.multiple_of(ahead * 128, 128), 128)]
    lane = lax.broadcasted_iota(jnp.int32, (1, 128), 1)
    crossing = jnp.where(lane < C, pltpu.roll(here, C, 1), pltpu.roll(after, C, 1))
    start = jnp.where(block - 1 < 0, pltpu.roll(here, C, 1), here)
    return jnp.where(first % 2 == 0, start, crossing)


def live_pair(doc_ref, query_block, key_block):
    row = lax.broadcasted_iota(jnp.int32, (C, 128), 0)
    lane = lax.broadcasted_iota(jnp.int32, (C, 128), 1)
    own = doc_pair(doc_ref, query_block)
    query_doc = jnp.sum(jnp.where(lane == row + C, own, 0), axis=1, keepdims=True)
    key_doc = doc_pair(doc_ref, key_block)
    key_pos = (key_block - 1) * C + lane
    query_pos = query_block * C + row
    return (key_doc == query_doc) & (key_pos <= query_pos) & (key_pos >= 0)


def attend(q_ref, g_ref, o_ref, lse_ref, keys, values, live, kv_acc, write_query):
    heads = q_ref.shape[1] // HD
    group = min(4, heads)
    row = lax.broadcasted_iota(jnp.int32, (C, 128), 0)
    lane = lax.broadcasted_iota(jnp.int32, (C, 128), 1)

    def step(at, carry):
        lanes = pl.ds(pl.multiple_of(at * group * HD, group * HD), group * HD)
        for half in range(2):
            rows = slice(half * C, half * C + C)

            def stacked(ref):
                wide = ref[rows, lanes]
                return jnp.concatenate([wide[:, i * HD : (i + 1) * HD] for i in range(group)], axis=0)

            q, g, o = stacked(q_ref), stacked(g_ref), stacked(o_ref)
            delta = jnp.sum(g.astype(F32) * o.astype(F32), axis=1, keepdims=True)
            lse = jnp.concatenate(
                [
                    jnp.sum(
                        jnp.where(lane == row + half * C, lse_ref[pl.ds(at * group + i, 1), :], 0.0),
                        axis=1,
                        keepdims=True,
                    )
                    for i in range(group)
                ],
                axis=0,
            )
            k, v = keys[half], values[half]
            dims = (((1,), (1,)), ((), ()))
            s = lax.dot_general(q, k, dims, preferred_element_type=F32)
            mask = jnp.concatenate([live[half]] * group, axis=0)
            p = jnp.where(mask > 0.0, jnp.exp(s * SCALE - lse), 0.0)
            dp = lax.dot_general(g, v, dims, preferred_element_type=F32)
            ds = (p * (dp - delta)).astype(BF)
            dq = jnp.dot(ds, k, preferred_element_type=F32) * SCALE
            tdims = (((0,), (0,)), ((), ()))
            dk = lax.dot_general(ds, q, tdims, preferred_element_type=F32) * SCALE
            dv = lax.dot_general(p.astype(BF), g, tdims, preferred_element_type=F32)
            kv_acc[half, :, :HD] += dk
            kv_acc[half, :, HD:] += dv
            wide = jnp.concatenate([dq[i * C : (i + 1) * C] for i in range(group)], axis=1)
            write_query(rows, lanes, wide)
        return carry

    kv_acc[...] = jnp.zeros_like(kv_acc)
    lax.fori_loop(0, heads // group, step, 0)


def pick(where, a, b):
    return jnp.where(where, a.astype(F32), b.astype(F32))


def pack_kernel(k_ref, v_ref, out_ref):
    out_ref[:, :HD] = k_ref[0]
    out_ref[:, HD:] = v_ref[0]


def widen_kernel(count, idx_ref, own_ref, left_ref, right_ref, low_ref, high_ref):
    last = idx_ref[0] == count - 1
    low_ref[:C] = left_ref[:C]
    low_ref[C:] = own_ref[:C]
    high_ref[:C] = pick(last, own_ref[:C], right_ref[C:]).astype(BF)
    high_ref[C:] = own_ref[C:]


def near_kernel(
    count, idx_ref, q_ref, g_ref, o_ref, lse_ref, doc_ref, low_ref, high_ref, dq_ref, kv_ref, live_ref
):
    place = idx_ref[0]
    for half, block in enumerate((place, 2 * count - 1 - place)):
        live_ref[half] = live_pair(doc_ref, block, block).astype(F32)
    keys = (low_ref[:, :HD], high_ref[:, :HD])
    values = (low_ref[:, HD:], high_ref[:, HD:])

    def write(rows, lanes, value):
        dq_ref[rows, lanes] = value

    attend(q_ref, g_ref, o_ref, lse_ref, keys, values, live_ref, kv_ref, write)


def far_kernel(
    count,
    idx_ref,
    q_ref,
    g_ref,
    o_ref,
    lse_ref,
    doc_ref,
    own_ref,
    left_ref,
    right_ref,
    left2_ref,
    right2_ref,
    near_ref,
    dq_ref,
    low_ref,
    high_ref,
    live_ref,
    acc_ref,
):
    place = idx_ref[0]
    last, before = place == count - 1, place == count - 2
    for half, block in enumerate((place, 2 * count - 1 - place)):
        live_ref[half] = live_pair(doc_ref, block, block - 2).astype(F32)
    third = pick(before, own_ref[:C], pick(last, left2_ref[C:], right2_ref[:C])).astype(BF)
    second = pick(before, right_ref[:C], pick(last, left_ref[:C], right2_ref[C:])).astype(BF)
    upper = jnp.concatenate([third, second], axis=0)
    keys = (left2_ref[:, :HD], upper[:, :HD])
    values = (left2_ref[:, HD:], upper[:, HD:])

    def write(rows, lanes, value):
        dq_ref[0, rows, lanes] = (value + near_ref[rows, lanes]).astype(BF)

    attend(q_ref, g_ref, o_ref, lse_ref, keys, values, live_ref, acc_ref, write)
    low_ref[:C] = acc_ref[0, :C].astype(BF)
    low_ref[C:] = (acc_ref[0, C:] + jnp.where(last, acc_ref[1, :C], 0.0)).astype(BF)
    high_ref[...] = acc_ref[1].astype(BF)


def turn_kernel(count, idx_ref, kv_ref, high_ref, low2_ref, high2_ref, left_ref, right_ref):
    last = idx_ref[0] == count - 1
    mine = jnp.where(last, high_ref[C:].astype(F32), 0.0)
    left_ref[...] = (kv_ref[0, :C] + low2_ref[:C].astype(F32) + mine).astype(BF)
    right_ref[:C] = (kv_ref[1, :C] + high2_ref[:C].astype(F32)).astype(BF)
    right_ref[C:] = high_ref[C:]


def close_kernel(
    count,
    idx_ref,
    kv_ref,
    high_ref,
    low2_ref,
    high2_ref,
    right_ref,
    low1_ref,
    high1_ref,
    dk_ref,
    dv_ref,
    spread_ref,
):
    place = idx_ref[0]
    last, before = place == count - 1, place == count - 2
    lower = kv_ref[0, C:] + low2_ref[C:].astype(F32) + low1_ref[...].astype(F32)
    lower += jnp.where(last, high1_ref[C:].astype(F32) + right_ref[:C].astype(F32), 0.0)
    lower += jnp.where(before, high_ref[:C].astype(F32), 0.0)
    upper = kv_ref[1, C:] + high2_ref[C:].astype(F32) + high1_ref[:C].astype(F32)
    both = jnp.concatenate([lower, upper], axis=0).astype(BF)
    dk_ref[0] = both[:, :HD]
    dv_ref[0] = both[:, HD:]
    for i in range(spread_ref.shape[0]):
        spread_ref[i] = both[:, HD:]


def chunk_kernel(x_ref, out_ref, sems):
    parts, _, width = out_ref.shape
    copies = [
        pltpu.make_async_copy(x_ref.at[0, :, pl.ds(i * width, width)], out_ref.at[i], sems.at[i])
        for i in range(parts)
    ]
    for copy in copies:
        copy.start()
    for copy in copies:
        copy.wait()


def weight_kernel(scale, x_ref, dv_ref, out_ref):
    parts, tokens, width = x_ref.shape
    x = x_ref[...].reshape(parts * tokens, width)
    dv = dv_ref[...].reshape(parts * tokens, HD)
    flat = lax.dot_general(dv, x, (((0,), (0,)), ((), ())), preferred_element_type=F32) * scale
    out_ref[...] = flat.T.astype(BF).reshape(out_ref.shape)


def shift(value, by):
    count = lax.axis_size(CTX)
    if by > 0:
        pairs = [(i, i + by) for i in range(count - by)]
    else:
        pairs = [(i - by, i) for i in range(count + by)]
    return lax.ppermute(value, CTX, pairs)


def body(layer_input, queries, key_heads, value_heads, attn_out, out_grad, log_sums, doc_ids):
    count = lax.axis_size(CTX)
    place = lax.axis_index(CTX).astype(jnp.int32).reshape(1)
    width = queries.shape[2]
    rows = 2 * C
    groups = lax.axis_size(ROWS)
    steps = lax.axis_size("ctx_1")
    heads = width // HD
    attend_flops = 10 * rows * 128 * HD * heads
    q, g, o, lse = queries[0], out_grad[0], attn_out[0], log_sums[0]
    at = functools.partial

    kv = pl.pallas_call(
        pack_kernel, out_shape=shape((rows, 2 * HD), BF), in_specs=[VMEM] * 2, out_specs=VMEM
    )(key_heads, value_heads)
    left = shift(kv, 1)
    right = shift(kv, -1)
    chunks = pl.pallas_call(
        chunk_kernel,
        out_shape=shape((groups, rows, layer_input.shape[2] // groups), BF),
        in_specs=[pl.BlockSpec(memory_space=pl.ANY)],
        out_specs=pl.BlockSpec(memory_space=pl.ANY),
        scratch_shapes=[pltpu.SemaphoreType.DMA((groups,))],
    )(layer_input)
    tokens = lax.all_to_all(chunks, ROWS, 0, 0, tiled=True)
    pair = shape((rows, 2 * HD), BF)
    low, high = call(at(widen_kernel, count), [pair, pair], 4, 0)(place, kv, left, right)
    left2 = shift(low, 2)
    right2 = shift(high, -2)
    near_query, near_kv = call(
        at(near_kernel, count),
        [shape((rows, width), F32), shape((2, 128, 2 * HD), F32)],
        8,
        attend_flops,
        [pltpu.VMEM((2, C, 128), F32)],
    )(place, q, g, o, lse, doc_ids, low, high)
    query_grad, far_low, far_high = call(
        at(far_kernel, count),
        [shape((1, rows, width), BF), pair, pair],
        12,
        attend_flops,
        [pltpu.VMEM((2, C, 128), F32), pltpu.VMEM((2, 128, 2 * HD), F32)],
    )(place, q, g, o, lse, doc_ids, kv, left, right, left2, right2, near_query)
    low2 = shift(far_low, -2)
    high2 = shift(far_high, 2)
    to_left, to_right = call(at(turn_kernel, count), [shape((C, 2 * HD), BF), pair], 5, 0)(
        place, near_kv, far_high, low2, high2
    )
    low1 = shift(to_left, -1)
    high1 = shift(to_right, 1)
    key_grad, value_grad, spread = call(
        at(close_kernel, count),
        [shape((1, rows, HD), BF), shape((1, rows, HD), BF), shape((groups, rows, HD), BF)],
        8,
        0,
    )(place, near_kv, far_high, low2, high2, to_right, low1, high1)
    spread, tokens = lax.optimization_barrier((spread, tokens))
    everyone = lax.all_to_all(spread, ROWS, 0, 0, tiled=True)
    weight_scale = (lax.axis_size("dp") * doc_ids.shape[1]) ** (-0.5)
    part = pl.pallas_call(
        at(weight_kernel, weight_scale),
        out_shape=shape((steps, tokens.shape[2] // steps, HD), BF),
        in_specs=[VMEM] * 2,
        out_specs=VMEM,
        compiler_params=pltpu.CompilerParams(vmem_limit_bytes=40 * 1024 * 1024),
    )(tokens, everyone)
    parts = lax.all_to_all(part, "ctx_1", 0, 0, tiled=True)
    weight_grad = jnp.sum(parts.astype(F32), axis=0)
    return (query_grad, key_grad, value_grad, weight_grad)


def solution(mesh):
    tall = 2 if mesh.shape["ctx"] % 2 == 0 else 1
    split = Mesh(
        mesh.devices.reshape(mesh.shape["dp"], tall, mesh.shape["ctx"] // tall, mesh.shape["tp"]),
        ("dp", "ctx_0", "ctx_1", "tp"),
    )
    in_specs = (
        P("dp", CTX, None),
        P("dp", CTX, "tp"),
        P("dp", CTX, "tp"),
        P("dp", CTX, "tp"),
        P("dp", CTX, "tp"),
        P("dp", CTX, "tp"),
        P("dp", "tp", CTX),
        P("dp", None),
    )
    out_specs = (P("dp", CTX, "tp"), P("dp", CTX, "tp"), P("dp", CTX, "tp"), P(DP_CTX, "tp"))
    return jax.shard_map(body, mesh=split, in_specs=in_specs, out_specs=out_specs, check_vma=False)
```

```python
import functools

import jax
import jax.numpy as jnp
from jax import lax
from jax.experimental import pallas as pl
from jax.experimental.pallas import tpu as pltpu
from jax.sharding import Mesh
from jax.sharding import PartitionSpec as P

HD = 128
C = 64
CTX = ("ctx_0", "ctx_1")
ROWS = ("dp", "ctx_0")
DP_CTX = ("dp", "ctx_0", "ctx_1")
SCALE = HD ** (-0.5)
BF = jnp.bfloat16
F32 = jnp.float32
SMEM = pl.BlockSpec(memory_space=pltpu.SMEM)
VMEM = pl.BlockSpec(memory_space=pltpu.VMEM)


def call(kernel, outs, n_in, flops, scratch=()):
    return pl.pallas_call(
        kernel,
        out_shape=outs,
        in_specs=[SMEM] + [VMEM] * (n_in - 1),
        out_specs=[VMEM] * len(outs),
        scratch_shapes=list(scratch),
        compiler_params=pltpu.CompilerParams(vmem_limit_bytes=40 * 1024 * 1024),
        cost_estimate=pl.CostEstimate(flops=flops, bytes_accessed=1 << 20, transcendentals=0),
    )


def shape(dims, dtype):
    return jax.ShapeDtypeStruct(dims, dtype)


def doc_pair(doc_ref, block):
    first = jnp.maximum(block - 1, 0)
    chunk = first // 2
    ahead = jnp.minimum(chunk + 1, doc_ref.shape[1] // 128 - 1)
    here = doc_ref[:, pl.ds(pl.multiple_of(chunk * 128, 128), 128)]
    after = doc_ref[:, pl.ds(pl.multiple_of(ahead * 128, 128), 128)]
    lane = lax.broadcasted_iota(jnp.int32, (1, 128), 1)
    crossing = jnp.where(lane < C, pltpu.roll(here, C, 1), pltpu.roll(after, C, 1))
    start = jnp.where(block - 1 < 0, pltpu.roll(here, C, 1), here)
    return jnp.where(first % 2 == 0, start, crossing)


def live_pair(doc_ref, query_block, key_block):
    row = lax.broadcasted_iota(jnp.int32, (C, 128), 0)
    lane = lax.broadcasted_iota(jnp.int32, (C, 128), 1)
    own = doc_pair(doc_ref, query_block)
    query_doc = jnp.sum(jnp.where(lane == row + C, own, 0), axis=1, keepdims=True)
    key_doc = doc_pair(doc_ref, key_block)
    key_pos = (key_block - 1) * C + lane
    query_pos = query_block * C + row
    return (key_doc == query_doc) & (key_pos <= query_pos) & (key_pos >= 0)


def attend(q_ref, g_ref, keys, values, live, kv_acc, lse_rows, delta_rows, write_query):
    heads = q_ref.shape[1] // HD
    group = min(4, heads)

    def step(at, carry):
        lanes = pl.ds(pl.multiple_of(at * group * HD, group * HD), group * HD)
        for half in range(2):
            rows = slice(half * C, half * C + C)

            def stacked(ref):
                wide = ref[rows, lanes]
                return jnp.concatenate([wide[:, i * HD : (i + 1) * HD] for i in range(group)], axis=0)

            q, g = stacked(q_ref), stacked(g_ref)
            lse, delta = lse_rows[half, at], delta_rows[half, at]
            k, v = keys[half], values[half]
            dims = (((1,), (1,)), ((), ()))
            s = lax.dot_general(q, k, dims, preferred_element_type=F32)
            mask = jnp.concatenate([live[half]] * group, axis=0)
            p = jnp.where(mask > 0.0, jnp.exp(s * SCALE - lse), 0.0)
            dp = lax.dot_general(g, v, dims, preferred_element_type=F32)
            ds = (p * (dp - delta)).astype(BF)
            dq = jnp.dot(ds, k, preferred_element_type=F32) * SCALE
            tdims = (((0,), (0,)), ((), ()))
            dk = lax.dot_general(ds, q, tdims, preferred_element_type=F32) * SCALE
            dv = lax.dot_general(p.astype(BF), g, tdims, preferred_element_type=F32)
            kv_acc[half, :, :HD] += dk
            kv_acc[half, :, HD:] += dv
            wide = jnp.concatenate([dq[i * C : (i + 1) * C] for i in range(group)], axis=1)
            write_query(rows, lanes, wide)
        return carry

    kv_acc[...] = jnp.zeros_like(kv_acc)
    lax.fori_loop(0, heads // group, step, 0)


def pick(where, a, b):
    return jnp.where(where, a.astype(F32), b.astype(F32))


def pack_kernel(k_ref, v_ref, out_ref):
    out_ref[:, :HD] = k_ref[0]
    out_ref[:, HD:] = v_ref[0]


def widen_kernel(count, idx_ref, k_ref, v_ref, left_ref, right_ref, low_ref, high_ref):
    last = idx_ref[0] == count - 1
    low_ref[:C] = left_ref[:C]
    for own_ref, lanes in ((k_ref, slice(0, HD)), (v_ref, slice(HD, 2 * HD))):
        low_ref[C:, lanes] = own_ref[0, :C]
        high_ref[:C, lanes] = pick(last, own_ref[0, :C], right_ref[C:, lanes]).astype(BF)
        high_ref[C:, lanes] = own_ref[0, C:]


def prepare_kernel(count, idx_ref, g_ref, o_ref, lse_ref, doc_ref, lse_rows, delta_rows, live_ref):
    place = idx_ref[0]
    for half, block in enumerate((place, 2 * count - 1 - place)):
        live_ref[0, half] = live_pair(doc_ref, block, block).astype(F32)
        live_ref[1, half] = live_pair(doc_ref, block, block - 2).astype(F32)
    row = lax.broadcasted_iota(jnp.int32, (C, 128), 0)
    lane = lax.broadcasted_iota(jnp.int32, (C, 128), 1)
    group = lse_rows.shape[2] // C

    def step(at, carry):
        for half in range(2):
            rows = slice(half * C, half * C + C)
            for i in range(group):
                head = at * group + i
                lanes = pl.ds(pl.multiple_of(head * HD, HD), HD)
                g, o = g_ref[rows, lanes].astype(F32), o_ref[rows, lanes].astype(F32)
                delta = jnp.sum(g * o, axis=1, keepdims=True)
                mine = jnp.where(lane == row + half * C, lse_ref[pl.ds(head, 1), :], 0.0)
                lse = jnp.sum(mine, axis=1, keepdims=True)
                into = slice(i * C, i * C + C)
                delta_rows[half, at, into] = jnp.broadcast_to(delta, (C, 128))
                lse_rows[half, at, into] = jnp.broadcast_to(lse, (C, 128))
        return carry

    lax.fori_loop(0, lse_rows.shape[1], step, 0)


def near_kernel(idx_ref, q_ref, g_ref, low_ref, high_ref, lse_rows, delta_rows, live_ref, dq_ref, kv_ref):
    keys = (low_ref[:, :HD], high_ref[:, :HD])
    values = (low_ref[:, HD:], high_ref[:, HD:])

    def write(rows, lanes, value):
        dq_ref[rows, lanes] = value

    attend(q_ref, g_ref, keys, values, live_ref[0], kv_ref, lse_rows, delta_rows, write)


def far_kernel(
    count,
    idx_ref,
    q_ref,
    g_ref,
    near_low_ref,
    right_ref,
    left2_ref,
    right2_ref,
    near_ref,
    lse_rows,
    delta_rows,
    live_ref,
    dq_ref,
    low_ref,
    high_ref,
    acc_ref,
):
    place = idx_ref[0]
    last, before = place == count - 1, place == count - 2
    third = pick(before, near_low_ref[C:], pick(last, left2_ref[C:], right2_ref[:C])).astype(BF)
    second = pick(before, right_ref[:C], pick(last, near_low_ref[:C], right2_ref[C:])).astype(BF)
    upper = jnp.concatenate([third, second], axis=0)
    keys = (left2_ref[:, :HD], upper[:, :HD])
    values = (left2_ref[:, HD:], upper[:, HD:])

    def write(rows, lanes, value):
        dq_ref[0, rows, lanes] = (value + near_ref[rows, lanes]).astype(BF)

    attend(q_ref, g_ref, keys, values, live_ref[1], acc_ref, lse_rows, delta_rows, write)
    low_ref[:C] = acc_ref[0, :C].astype(BF)
    low_ref[C:] = (acc_ref[0, C:] + jnp.where(last, acc_ref[1, :C], 0.0)).astype(BF)
    high_ref[...] = acc_ref[1].astype(BF)


def turn_kernel(count, idx_ref, kv_ref, high_ref, low2_ref, high2_ref, left_ref, right_ref):
    last = idx_ref[0] == count - 1
    mine = jnp.where(last, high_ref[C:].astype(F32), 0.0)
    left_ref[...] = (kv_ref[0, :C] + low2_ref[:C].astype(F32) + mine).astype(BF)
    right_ref[:C] = (kv_ref[1, :C] + high2_ref[:C].astype(F32)).astype(BF)
    right_ref[C:] = high_ref[C:]


def close_kernel(
    count,
    idx_ref,
    kv_ref,
    high_ref,
    low2_ref,
    high2_ref,
    right_ref,
    low1_ref,
    high1_ref,
    dk_ref,
    dv_ref,
    spread_ref,
):
    place = idx_ref[0]
    last, before = place == count - 1, place == count - 2
    lower = kv_ref[0, C:] + low2_ref[C:].astype(F32) + low1_ref[...].astype(F32)
    lower += jnp.where(last, high1_ref[C:].astype(F32) + right_ref[:C].astype(F32), 0.0)
    lower += jnp.where(before, high_ref[:C].astype(F32), 0.0)
    upper = kv_ref[1, C:] + high2_ref[C:].astype(F32) + high1_ref[:C].astype(F32)
    both = jnp.concatenate([lower, upper], axis=0).astype(BF)
    dk_ref[0] = both[:, :HD]
    dv_ref[0] = both[:, HD:]
    for i in range(spread_ref.shape[0]):
        spread_ref[i] = both[:, HD:]


def chunk_kernel(tp_ref, x_ref, out_ref, sems):
    parts, _, width = out_ref.shape
    stride = x_ref.shape[2] // parts
    copies = []
    for i in range(parts):
        lanes = pl.ds(pl.multiple_of(i * stride + tp_ref[0] * width, 128), width)
        copies.append(pltpu.make_async_copy(x_ref.at[0, :, lanes], out_ref.at[i], sems.at[i]))
    for copy in copies:
        copy.start()
    for copy in copies:
        copy.wait()


def repeat_kernel(x_ref, out_ref):
    for i in range(out_ref.shape[0]):
        out_ref[i] = x_ref[...]


def weight_kernel(scale, x_ref, dv_ref, out_ref):
    pieces, parts, tokens, width = x_ref.shape
    each = out_ref.shape[0] // pieces
    dv = dv_ref[...].reshape(parts * tokens, HD).T
    for i in range(pieces):
        x = x_ref[i].reshape(parts * tokens, width)
        flat = jnp.dot(dv, x, preferred_element_type=F32) * scale
        out_ref[i * each : (i + 1) * each] = flat.T.astype(BF).reshape(each, width // each, HD)


def shift(value, by):
    count = lax.axis_size(CTX)
    if by > 0:
        pairs = [(i, i + by) for i in range(count - by)]
    else:
        pairs = [(i - by, i) for i in range(count + by)]
    return lax.ppermute(value, CTX, pairs)


def body(layer_input, queries, key_heads, value_heads, attn_out, out_grad, log_sums, doc_ids):
    count = lax.axis_size(CTX)
    place = lax.axis_index(CTX).astype(jnp.int32).reshape(1)
    width = queries.shape[2]
    rows = 2 * C
    groups = lax.axis_size(ROWS)
    steps = lax.axis_size("ctx_1")
    heads = width // HD
    attend_flops = 10 * rows * 128 * HD * heads
    q, g, o, lse = queries[0], out_grad[0], attn_out[0], log_sums[0]
    at = functools.partial

    kv = pl.pallas_call(
        pack_kernel, out_shape=shape((rows, 2 * HD), BF), in_specs=[VMEM] * 2, out_specs=VMEM
    )(key_heads, value_heads)
    left = shift(kv, 1)
    right = shift(kv, -1)
    group = min(4, heads)
    row_terms = shape((2, heads // group, group * C, 128), F32)
    lse_rows, delta_rows, live = call(
        at(prepare_kernel, count), [row_terms, row_terms, shape((2, 2, C, 128), F32)], 5, attend_flops
    )(place, g, o, lse, doc_ids)
    left, lse_rows = lax.optimization_barrier((left, lse_rows))
    pieces = lax.axis_size("tp")
    piece = layer_input.shape[2] // (groups * pieces)
    chunks = pl.pallas_call(
        chunk_kernel,
        out_shape=shape((groups, rows, piece), BF),
        in_specs=[SMEM, pl.BlockSpec(memory_space=pl.ANY)],
        out_specs=VMEM,
        scratch_shapes=[pltpu.SemaphoreType.DMA((groups,))],
    )(lax.axis_index("tp").astype(jnp.int32).reshape(1), layer_input)
    mine = lax.all_to_all(chunks, ROWS, 0, 0, tiled=True)
    pair = shape((rows, 2 * HD), BF)
    low, high = call(at(widen_kernel, count), [pair, pair], 5, 0)(place, key_heads, value_heads, left, right)
    left2 = shift(low, 2)
    right2 = shift(high, -2)
    low, high, mine = lax.optimization_barrier((low, high, mine))
    repeated = pl.pallas_call(
        repeat_kernel, out_shape=shape((pieces, groups, rows, piece), BF), in_specs=[VMEM], out_specs=VMEM
    )(mine)
    tokens = lax.all_to_all(repeated, "tp", 0, 0, tiled=True)
    near_query, near_kv = call(
        near_kernel,
        [shape((rows, width), F32), shape((2, 128, 2 * HD), F32)],
        8,
        attend_flops,
    )(place, q, g, low, high, lse_rows, delta_rows, live)
    query_grad, far_low, far_high = call(
        at(far_kernel, count),
        [shape((1, rows, width), BF), pair, pair],
        11,
        attend_flops,
        [pltpu.VMEM((2, 128, 2 * HD), F32)],
    )(place, q, g, low, right, left2, right2, near_query, lse_rows, delta_rows, live)
    low2 = shift(far_low, -2)
    high2 = shift(far_high, 2)
    to_left, to_right = call(at(turn_kernel, count), [shape((C, 2 * HD), BF), pair], 5, 0)(
        place, near_kv, far_high, low2, high2
    )
    low1 = shift(to_left, -1)
    high1 = shift(to_right, 1)
    key_grad, value_grad, spread = call(
        at(close_kernel, count),
        [shape((1, rows, HD), BF), shape((1, rows, HD), BF), shape((groups, rows, HD), BF)],
        8,
        0,
    )(place, near_kv, far_high, low2, high2, to_right, low1, high1)
    spread, tokens = lax.optimization_barrier((spread, tokens))
    everyone = lax.all_to_all(spread, ROWS, 0, 0, tiled=True)
    weight_scale = (lax.axis_size("dp") * doc_ids.shape[1]) ** (-0.5)
    part = pl.pallas_call(
        at(weight_kernel, weight_scale),
        out_shape=shape((steps, piece * pieces // steps, HD), BF),
        in_specs=[VMEM] * 2,
        out_specs=VMEM,
        compiler_params=pltpu.CompilerParams(vmem_limit_bytes=40 * 1024 * 1024),
    )(tokens, everyone)
    parts = lax.all_to_all(part, "ctx_1", 0, 0, tiled=True)
    weight_grad = jnp.sum(parts.astype(F32), axis=0)
    return (query_grad, key_grad, value_grad, weight_grad)


def solution(mesh):
    tall = 2 if mesh.shape["ctx"] % 2 == 0 else 1
    split = Mesh(
        mesh.devices.reshape(mesh.shape["dp"], tall, mesh.shape["ctx"] // tall, mesh.shape["tp"]),
        ("dp", "ctx_0", "ctx_1", "tp"),
    )
    in_specs = (
        P("dp", CTX, None),
        P("dp", CTX, "tp"),
        P("dp", CTX, "tp"),
        P("dp", CTX, "tp"),
        P("dp", CTX, "tp"),
        P("dp", CTX, "tp"),
        P("dp", "tp", CTX),
        P("dp", None),
    )
    out_specs = (P("dp", CTX, "tp"), P("dp", CTX, "tp"), P("dp", CTX, "tp"), P(DP_CTX, "tp"))
    return jax.shard_map(body, mesh=split, in_specs=in_specs, out_specs=out_specs, check_vma=False)
```

```python
import functools

import jax
import jax.numpy as jnp
from jax import lax
from jax.experimental import pallas as pl
from jax.experimental.pallas import tpu as pltpu
from jax.sharding import Mesh
from jax.sharding import PartitionSpec as P

HD = 128
C = 64
CTX = ("ctx_0", "ctx_1")
ROWS = ("dp", "ctx_0")
DP_CTX = ("dp", "ctx_0", "ctx_1")
SCALE = HD ** (-0.5)
BF = jnp.bfloat16
F32 = jnp.float32
SMEM = pl.BlockSpec(memory_space=pltpu.SMEM)
VMEM = pl.BlockSpec(memory_space=pltpu.VMEM)
COST = {"prepare": 1, "widen": 0.1, "near": 3, "far": 3, "turn": 10, "close": 10}


def call(kernel, outs, in_specs, us, scratch=(), mib=8):
    return pl.pallas_call(
        kernel,
        name=getattr(kernel, "func", kernel).__name__,
        out_shape=outs,
        in_specs=in_specs,
        out_specs=[VMEM] * len(outs),
        scratch_shapes=list(scratch),
        compiler_params=pltpu.CompilerParams(vmem_limit_bytes=mib * 1024 * 1024),
        cost_estimate=pl.CostEstimate(flops=int(us * 1e9), bytes_accessed=0, transcendentals=0),
    )


def shape(dims, dtype):
    return jax.ShapeDtypeStruct(dims, dtype)


def doc_pair(doc_ref, block):
    first = jnp.maximum(block - 1, 0)
    chunk = first // 2
    ahead = jnp.minimum(chunk + 1, doc_ref.shape[1] // 128 - 1)
    here = doc_ref[:, pl.ds(pl.multiple_of(chunk * 128, 128), 128)]
    after = doc_ref[:, pl.ds(pl.multiple_of(ahead * 128, 128), 128)]
    lane = lax.broadcasted_iota(jnp.int32, (1, 128), 1)
    crossing = jnp.where(lane < C, pltpu.roll(here, C, 1), pltpu.roll(after, C, 1))
    start = jnp.where(block - 1 < 0, pltpu.roll(here, C, 1), here)
    return jnp.where(first % 2 == 0, start, crossing)


def live_pair(doc_ref, query_block, key_block):
    row = lax.broadcasted_iota(jnp.int32, (C, 128), 0)
    lane = lax.broadcasted_iota(jnp.int32, (C, 128), 1)
    own = doc_pair(doc_ref, query_block)
    query_doc = jnp.sum(jnp.where(lane == row + C, own, 0), axis=1, keepdims=True)
    key_doc = doc_pair(doc_ref, key_block)
    key_pos = (key_block - 1) * C + lane
    query_pos = query_block * C + row
    return (key_doc == query_doc) & (key_pos <= query_pos) & (key_pos >= 0)


def attend(q_rows, g_rows, keys, values, live, kv_acc, lse_rows, delta_rows, write_query):
    steps, group = q_rows.shape[1], q_rows.shape[2] // C

    def step(at, carry):
        lanes = pl.ds(pl.multiple_of(at * group * HD, group * HD), group * HD)
        for half in range(2):
            rows = slice(half * C, half * C + C)
            q, g = q_rows[half, at], g_rows[half, at]
            lse, delta = lse_rows[half, at], delta_rows[half, at]
            k, v = keys[half], values[half]
            dims = (((1,), (1,)), ((), ()))
            s = lax.dot_general(q, k, dims, preferred_element_type=F32)
            mask = jnp.concatenate([live[half]] * group, axis=0)
            p = jnp.where(mask > 0.0, jnp.exp(s * SCALE - lse), 0.0)
            dp = lax.dot_general(g, v, dims, preferred_element_type=F32)
            ds = (p * (dp - delta)).astype(BF)
            dq = jnp.dot(ds, k, preferred_element_type=F32) * SCALE
            tdims = (((0,), (0,)), ((), ()))
            dk = lax.dot_general(ds, q, tdims, preferred_element_type=F32) * SCALE
            dv = lax.dot_general(p.astype(BF), g, tdims, preferred_element_type=F32)
            kv_acc[half, :, :HD] += dk
            kv_acc[half, :, HD:] += dv
            wide = jnp.concatenate([dq[i * C : (i + 1) * C] for i in range(group)], axis=1)
            write_query(rows, lanes, wide)
        return carry

    kv_acc[...] = jnp.zeros_like(kv_acc)
    lax.fori_loop(0, steps, step, 0)


def pick(where, a, b):
    return jnp.where(where, a.astype(F32), b.astype(F32))


def pack_kernel(k_ref, v_ref, out_ref):
    out_ref[:, :HD] = k_ref[0]
    out_ref[:, HD:] = v_ref[0]


def widen_kernel(count, idx_ref, k_ref, v_ref, left_ref, right_ref, low_ref, high_ref):
    last = idx_ref[0] == count - 1
    low_ref[:C] = left_ref[:C]
    for own_ref, lanes in ((k_ref, slice(0, HD)), (v_ref, slice(HD, 2 * HD))):
        low_ref[C:, lanes] = own_ref[0, :C]
        high_ref[:C, lanes] = pick(last, own_ref[0, :C], right_ref[C:, lanes]).astype(BF)
        high_ref[C:, lanes] = own_ref[0, C:]


def prepare_kernel(
    count, idx_ref, q_ref, g_ref, o_ref, lse_ref, doc_ref, q_rows, g_rows, lse_rows, delta_rows, live_ref
):
    place = idx_ref[0]
    for half, block in enumerate((place, 2 * count - 1 - place)):
        live_ref[0, half] = live_pair(doc_ref, block, block).astype(F32)
        live_ref[1, half] = live_pair(doc_ref, block, block - 2).astype(F32)
    row = lax.broadcasted_iota(jnp.int32, (C, 128), 0)
    lane = lax.broadcasted_iota(jnp.int32, (C, 128), 1)
    group = lse_rows.shape[2] // C

    def step(at, carry):
        for half in range(2):
            rows = slice(half * C, half * C + C)
            for i in range(group):
                head = at * group + i
                lanes = pl.ds(pl.multiple_of(head * HD, HD), HD)
                g = g_ref[rows, lanes]
                delta = jnp.sum(g.astype(F32) * o_ref[rows, lanes].astype(F32), axis=1, keepdims=True)
                mine = jnp.where(lane == row + half * C, lse_ref[pl.ds(head, 1), :], 0.0)
                lse = jnp.sum(mine, axis=1, keepdims=True)
                into = slice(i * C, i * C + C)
                q_rows[half, at, into] = q_ref[rows, lanes]
                g_rows[half, at, into] = g
                delta_rows[half, at, into] = jnp.broadcast_to(delta, (C, 128))
                lse_rows[half, at, into] = jnp.broadcast_to(lse, (C, 128))
        return carry

    lax.fori_loop(0, lse_rows.shape[1], step, 0)


def near_kernel(idx_ref, q_rows, g_rows, low_ref, high_ref, lse_rows, delta_rows, live_ref, dq_ref, kv_ref):
    keys = (low_ref[:, :HD], high_ref[:, :HD])
    values = (low_ref[:, HD:], high_ref[:, HD:])

    def write(rows, lanes, value):
        dq_ref[rows, lanes] = value

    attend(q_rows, g_rows, keys, values, live_ref[0], kv_ref, lse_rows, delta_rows, write)


def far_kernel(
    count,
    idx_ref,
    q_rows,
    g_rows,
    near_low_ref,
    right_ref,
    left2_ref,
    right2_ref,
    near_ref,
    lse_rows,
    delta_rows,
    live_ref,
    dq_ref,
    low_ref,
    high_ref,
    acc_ref,
):
    place = idx_ref[0]
    last, before = place == count - 1, place == count - 2
    third = pick(before, near_low_ref[C:], pick(last, left2_ref[C:], right2_ref[:C])).astype(BF)
    second = pick(before, right_ref[:C], pick(last, near_low_ref[:C], right2_ref[C:])).astype(BF)
    upper = jnp.concatenate([third, second], axis=0)
    keys = (left2_ref[:, :HD], upper[:, :HD])
    values = (left2_ref[:, HD:], upper[:, HD:])

    def write(rows, lanes, value):
        dq_ref[0, rows, lanes] = (value + near_ref[rows, lanes]).astype(BF)

    attend(q_rows, g_rows, keys, values, live_ref[1], acc_ref, lse_rows, delta_rows, write)
    low_ref[:C] = acc_ref[0, :C].astype(BF)
    low_ref[C:] = (acc_ref[0, C:] + jnp.where(last, acc_ref[1, :C], 0.0)).astype(BF)
    high_ref[...] = acc_ref[1].astype(BF)


def turn_kernel(count, idx_ref, kv_ref, high_ref, low2_ref, high2_ref, left_ref, right_ref):
    last = idx_ref[0] == count - 1
    mine = jnp.where(last, high_ref[C:].astype(F32), 0.0)
    left_ref[...] = (kv_ref[0, :C] + low2_ref[:C].astype(F32) + mine).astype(BF)
    right_ref[:C] = (kv_ref[1, :C] + high2_ref[:C].astype(F32)).astype(BF)
    right_ref[C:] = high_ref[C:]


def close_kernel(
    count,
    idx_ref,
    kv_ref,
    high_ref,
    low2_ref,
    high2_ref,
    right_ref,
    low1_ref,
    high1_ref,
    dk_ref,
    dv_ref,
    spread_ref,
):
    place = idx_ref[0]
    last, before = place == count - 1, place == count - 2
    lower = kv_ref[0, C:] + low2_ref[C:].astype(F32) + low1_ref[...].astype(F32)
    lower += jnp.where(last, high1_ref[C:].astype(F32) + right_ref[:C].astype(F32), 0.0)
    lower += jnp.where(before, high_ref[:C].astype(F32), 0.0)
    upper = kv_ref[1, C:] + high2_ref[C:].astype(F32) + high1_ref[:C].astype(F32)
    both = jnp.concatenate([lower, upper], axis=0).astype(BF)
    dk_ref[0] = both[:, :HD]
    dv_ref[0] = both[:, HD:]
    for i in range(spread_ref.shape[0]):
        spread_ref[i] = both[:, HD:]


def chunk_kernel(tp_ref, x_ref, out_ref, sems):
    parts, _, width = out_ref.shape
    stride = x_ref.shape[2] // parts
    copies = []
    for i in range(parts):
        lanes = pl.ds(pl.multiple_of(i * stride + tp_ref[0] * width, 128), width)
        copies.append(pltpu.make_async_copy(x_ref.at[0, :, lanes], out_ref.at[i], sems.at[i]))
    for copy in copies:
        copy.start()
    for copy in copies:
        copy.wait()


def repeat_kernel(x_ref, out_ref):
    for i in range(out_ref.shape[0]):
        out_ref[i] = x_ref[...]


def weight_kernel(scale, x_ref, dv_ref, out_ref):
    pieces, parts, tokens, width = x_ref.shape
    each = out_ref.shape[0] // pieces
    dv = dv_ref[...].reshape(parts * tokens, HD).T
    for i in range(pieces):
        x = x_ref[i].reshape(parts * tokens, width)
        flat = jnp.dot(dv, x, preferred_element_type=F32) * scale
        out_ref[i * each : (i + 1) * each] = flat.T.astype(BF).reshape(each, width // each, HD)


def shift(value, by):
    count = lax.axis_size(CTX)
    if by > 0:
        pairs = [(i, i + by) for i in range(count - by)]
    else:
        pairs = [(i - by, i) for i in range(count + by)]
    return lax.ppermute(value, CTX, pairs)


def body(layer_input, queries, key_heads, value_heads, attn_out, out_grad, log_sums, doc_ids):
    count = lax.axis_size(CTX)
    place = lax.axis_index(CTX).astype(jnp.int32).reshape(1)
    width = queries.shape[2]
    rows = 2 * C
    groups = lax.axis_size(ROWS)
    steps = lax.axis_size("ctx_1")
    pieces = lax.axis_size("tp")
    piece = layer_input.shape[2] // (groups * pieces)
    heads = width // HD
    group = min(4, heads)
    row_terms = shape((2, heads // group, group * C, 128), F32)
    head_rows = shape(row_terms.shape, BF)
    pair = shape((rows, 2 * HD), BF)
    at = functools.partial

    (kv,) = call(pack_kernel, [pair], [VMEM] * 2, 1, mib=56)(key_heads, value_heads)
    left = shift(kv, 1)
    right = shift(kv, -1)
    q_rows, g_rows, lse_rows, delta_rows, live = call(
        at(prepare_kernel, count),
        [head_rows, head_rows, row_terms, row_terms, shape((2, 2, C, 128), F32)],
        [SMEM] + [VMEM] * 5,
        COST["prepare"],
        mib=12,
    )(place, queries[0], out_grad[0], attn_out[0], log_sums[0], doc_ids)
    left, live = lax.optimization_barrier((left, live))
    (chunks,) = call(
        chunk_kernel,
        [shape((groups, rows, piece), BF)],
        [SMEM, pl.BlockSpec(memory_space=pl.ANY)],
        2,
        [pltpu.SemaphoreType.DMA((groups,))],
    )(lax.axis_index("tp").astype(jnp.int32).reshape(1), layer_input)
    mine = lax.all_to_all(chunks, ROWS, 0, 0, tiled=True)
    low, high = call(at(widen_kernel, count), [pair, pair], [SMEM] + [VMEM] * 4, COST["widen"])(
        place, key_heads, value_heads, left, right
    )
    left2 = shift(low, 2)
    right2 = shift(high, -2)
    near_query, near_kv = call(
        near_kernel,
        [shape((rows, width), F32), shape((2, 128, 2 * HD), F32)],
        [SMEM] + [VMEM] * 7,
        COST["near"],
        mib=12,
    )(place, q_rows, g_rows, low, high, lse_rows, delta_rows, live)
    query_grad, far_low, far_high = call(
        at(far_kernel, count),
        [shape((1, rows, width), BF), pair, pair],
        [SMEM] + [VMEM] * 10,
        COST["far"],
        [pltpu.VMEM((2, 128, 2 * HD), F32)],
        mib=12,
    )(place, q_rows, g_rows, low, right, left2, right2, near_query, lse_rows, delta_rows, live)
    low2 = shift(far_low, -2)
    high2 = shift(far_high, 2)
    low2, mine = lax.optimization_barrier((low2, mine))
    (repeated,) = call(repeat_kernel, [shape((pieces, groups, rows, piece), BF)], [VMEM], 2)(mine)
    tokens = lax.all_to_all(repeated, "tp", 0, 0, tiled=True)
    to_left, to_right = call(
        at(turn_kernel, count), [shape((C, 2 * HD), BF), pair], [SMEM] + [VMEM] * 4, COST["turn"]
    )(place, near_kv, far_high, low2, high2)
    low1 = shift(to_left, -1)
    high1 = shift(to_right, 1)
    grad = shape((1, rows, HD), BF)
    key_grad, value_grad, spread = call(
        at(close_kernel, count),
        [grad, grad, shape((groups, rows, HD), BF)],
        [SMEM] + [VMEM] * 7,
        COST["close"],
    )(place, near_kv, far_high, low2, high2, to_right, low1, high1)
    spread, tokens = lax.optimization_barrier((spread, tokens))
    everyone = lax.all_to_all(spread, ROWS, 0, 0, tiled=True)
    weight_scale = (lax.axis_size("dp") * doc_ids.shape[1]) ** (-0.5)
    (part,) = call(
        at(weight_kernel, weight_scale),
        [shape((steps, piece * pieces // steps, HD), BF)],
        [VMEM] * 2,
        1,
        mib=12,
    )(tokens, everyone)
    parts = lax.all_to_all(part, "ctx_1", 0, 0, tiled=True)
    weight_grad = jnp.sum(parts.astype(F32), axis=0)
    return (query_grad, key_grad, value_grad, weight_grad)


def solution(mesh):
    tall = 2 if mesh.shape["ctx"] % 2 == 0 else 1
    split = Mesh(
        mesh.devices.reshape(mesh.shape["dp"], tall, mesh.shape["ctx"] // tall, mesh.shape["tp"]),
        ("dp", "ctx_0", "ctx_1", "tp"),
    )
    in_specs = (
        P("dp", CTX, None),
        P("dp", CTX, "tp"),
        P("dp", CTX, "tp"),
        P("dp", CTX, "tp"),
        P("dp", CTX, "tp"),
        P("dp", CTX, "tp"),
        P("dp", "tp", CTX),
        P("dp", None),
    )
    out_specs = (P("dp", CTX, "tp"), P("dp", CTX, "tp"), P("dp", CTX, "tp"), P(DP_CTX, "tp"))
    return jax.shard_map(body, mesh=split, in_specs=in_specs, out_specs=out_specs, check_vma=False)
```

```python
import functools

import jax
import jax.numpy as jnp
from jax import lax
from jax.experimental import pallas as pl
from jax.experimental.pallas import tpu as pltpu
from jax.sharding import Mesh
from jax.sharding import PartitionSpec as P

HD = 128
C = 64
CTX = ("ctx_0", "ctx_1")
ROWS = ("dp", "ctx_0")
DP_CTX = ("dp", "ctx_0", "ctx_1")
TP = ("tp_x", "core")
SCALE = HD ** (-0.5)
BF = jnp.bfloat16
F32 = jnp.float32
SMEM = pl.BlockSpec(memory_space=pltpu.SMEM)
VMEM = pl.BlockSpec(memory_space=pltpu.VMEM)
ANY = pl.BlockSpec(memory_space=pl.ANY)
COST = {"prepare": 2, "widen": 0.1, "near": 0.3, "far": 0.3, "turn": 10, "close": 5, "finish": 0.5}


def call(kernel, outs, in_specs, us, scratch=(), mib=8):
    return pl.pallas_call(
        kernel,
        name=getattr(kernel, "func", kernel).__name__,
        out_shape=outs,
        in_specs=in_specs,
        out_specs=[VMEM] * len(outs),
        scratch_shapes=list(scratch),
        compiler_params=pltpu.CompilerParams(vmem_limit_bytes=mib * 1024 * 1024),
        cost_estimate=pl.CostEstimate(flops=int(us * 1e9), bytes_accessed=0, transcendentals=0),
    )


def shape(dims, dtype):
    return jax.ShapeDtypeStruct(dims, dtype)


def doc_pair(doc_ref, block):
    first = jnp.maximum(block - 1, 0)
    chunk = first // 2
    ahead = jnp.minimum(chunk + 1, doc_ref.shape[1] // 128 - 1)
    here = doc_ref[:, pl.ds(pl.multiple_of(chunk * 128, 128), 128)]
    after = doc_ref[:, pl.ds(pl.multiple_of(ahead * 128, 128), 128)]
    lane = lax.broadcasted_iota(jnp.int32, (1, 128), 1)
    crossing = jnp.where(lane < C, pltpu.roll(here, C, 1), pltpu.roll(after, C, 1))
    start = jnp.where(block - 1 < 0, pltpu.roll(here, C, 1), here)
    return jnp.where(first % 2 == 0, start, crossing)


def live_pair(doc_ref, query_block, key_block):
    row = lax.broadcasted_iota(jnp.int32, (C, 128), 0)
    lane = lax.broadcasted_iota(jnp.int32, (C, 128), 1)
    own = doc_pair(doc_ref, query_block)
    query_doc = jnp.sum(jnp.where(lane == row + C, own, 0), axis=1, keepdims=True)
    key_doc = doc_pair(doc_ref, key_block)
    key_pos = (key_block - 1) * C + lane
    query_pos = query_block * C + row
    return (key_doc == query_doc) & (key_pos <= query_pos) & (key_pos >= 0)


def attend(q_rows, g_rows, keys, values, live, kv_acc, lse_rows, delta_rows, write_query):
    steps, group = q_rows.shape[1], q_rows.shape[2] // C

    def step(at, carry):
        lanes = pl.ds(pl.multiple_of(at * group * HD, group * HD), group * HD)
        for half in range(2):
            rows = slice(half * C, half * C + C)
            q, g = q_rows[half, at], g_rows[half, at]
            lse, delta = lse_rows[half, at], delta_rows[half, at]
            k, v = keys[half], values[half]
            dims = (((1,), (1,)), ((), ()))
            s = lax.dot_general(q, k, dims, preferred_element_type=F32)
            mask = jnp.concatenate([live[half]] * group, axis=0)
            p = jnp.where(mask > 0.0, jnp.exp(s * SCALE - lse), 0.0)
            dp = lax.dot_general(g, v, dims, preferred_element_type=F32)
            ds = (p * (dp - delta)).astype(BF)
            dq = jnp.dot(ds, k, preferred_element_type=F32) * SCALE
            tdims = (((0,), (0,)), ((), ()))
            dk = lax.dot_general(ds, q, tdims, preferred_element_type=F32) * SCALE
            dv = lax.dot_general(p.astype(BF), g, tdims, preferred_element_type=F32)
            kv_acc[half, :, :HD] += dk
            kv_acc[half, :, HD:] += dv
            wide = jnp.concatenate([dq[i * C : (i + 1) * C] for i in range(group)], axis=1)
            write_query(rows, lanes, wide)
        return carry

    kv_acc[...] = jnp.zeros_like(kv_acc)
    lax.fori_loop(0, steps, step, 0)


def pick(where, a, b):
    return jnp.where(where, a.astype(F32), b.astype(F32))


def pack_kernel(count, idx_ref, k_ref, v_ref, kv_ref, cross_ref, k_buf, v_buf, sems):
    copies = [
        pltpu.make_async_copy(k_ref.at[0], k_buf, sems.at[0]),
        pltpu.make_async_copy(v_ref.at[0], v_buf, sems.at[1]),
    ]
    for copy in copies:
        copy.start()
    for copy in copies:
        copy.wait()
    kv_ref[:, :HD] = k_buf[...]
    kv_ref[:, HD:] = v_buf[...]
    first = idx_ref[0] < count // 2
    cross_ref[:, :HD] = pick(first, k_buf[:C], k_buf[C:]).astype(BF)
    cross_ref[:, HD:] = pick(first, v_buf[:C], v_buf[C:]).astype(BF)


def first_kernel(count, idx_ref, kv_ref, cross_ref, left_ref, right_ref):
    place = idx_ref[0]
    left_ref[:C] = pick(place == count - 1, cross_ref[...], kv_ref[:C]).astype(BF)
    left_ref[C:] = cross_ref[...]
    right_ref[:C] = kv_ref[:C]
    right_ref[C : 2 * C] = pick(place == 0, cross_ref[...], kv_ref[C:]).astype(BF)
    right_ref[2 * C :] = cross_ref[...]


def widen_kernel(
    count, idx_ref, kv_ref, cross_ref, left_ref, right_ref, low_ref, high_ref, send_low_ref, send_high_ref
):
    place = idx_ref[0]
    lower, upper, other = kv_ref[:C], kv_ref[C:], cross_ref[...]
    before_lower = left_ref[:C]
    before_upper = pick(place == count - 1, lower, right_ref[C : 2 * C]).astype(BF)
    low_ref[:C] = before_lower
    low_ref[C:] = lower
    high_ref[:C] = before_upper
    high_ref[C:] = upper
    end, start = place >= count - 2, place < 2
    send_low_ref[:C] = pick(end, left_ref[C:], before_lower).astype(BF)
    send_low_ref[C:] = pick(end, other, lower).astype(BF)
    send_high_ref[:C] = pick(start, right_ref[2 * C :], before_upper).astype(BF)
    send_high_ref[C:] = pick(start, other, upper).astype(BF)


def prepare_kernel(
    count, idx_ref, q_ref, g_ref, o_ref, lse_ref, doc_ref, q_rows, g_rows, lse_rows, delta_rows, live_ref
):
    place = idx_ref[0]
    for half, block in enumerate((place, 2 * count - 1 - place)):
        live_ref[0, half] = live_pair(doc_ref, block, block).astype(F32)
        live_ref[1, half] = live_pair(doc_ref, block, block - 2).astype(F32)
    row = lax.broadcasted_iota(jnp.int32, (C, 128), 0)
    lane = lax.broadcasted_iota(jnp.int32, (C, 128), 1)
    group = lse_rows.shape[2] // C

    def step(at, carry):
        for half in range(2):
            rows = slice(half * C, half * C + C)
            for i in range(group):
                head = at * group + i
                lanes = pl.ds(pl.multiple_of(head * HD, HD), HD)
                g = g_ref[rows, lanes]
                delta = jnp.sum(g.astype(F32) * o_ref[rows, lanes].astype(F32), axis=1, keepdims=True)
                mine = jnp.where(lane == row + half * C, lse_ref[pl.ds(head, 1), :], 0.0)
                lse = jnp.sum(mine, axis=1, keepdims=True)
                into = slice(i * C, i * C + C)
                q_rows[half, at, into] = q_ref[rows, lanes]
                g_rows[half, at, into] = g
                delta_rows[half, at, into] = jnp.broadcast_to(delta, (C, 128))
                lse_rows[half, at, into] = jnp.broadcast_to(lse, (C, 128))
        return carry

    lax.fori_loop(0, lse_rows.shape[1], step, 0)


def near_kernel(idx_ref, q_rows, g_rows, low_ref, high_ref, lse_rows, delta_rows, live_ref, dq_ref, kv_ref):
    keys = (low_ref[:, :HD], high_ref[:, :HD])
    values = (low_ref[:, HD:], high_ref[:, HD:])

    def write(rows, lanes, value):
        dq_ref[rows, lanes] = value

    attend(q_rows, g_rows, keys, values, live_ref[0], kv_ref, lse_rows, delta_rows, write)


def far_kernel(
    count,
    idx_ref,
    q_rows,
    g_rows,
    near_low_ref,
    right_ref,
    left2_ref,
    right2_ref,
    near_ref,
    lse_rows,
    delta_rows,
    live_ref,
    dq_ref,
    low_ref,
    high_ref,
    acc_ref,
):
    place = idx_ref[0]
    last, before = place == count - 1, place == count - 2
    third = pick(before, near_low_ref[C:], pick(last, left2_ref[C:], right2_ref[:C])).astype(BF)
    second = pick(before, right_ref[:C], pick(last, near_low_ref[:C], right2_ref[C:])).astype(BF)
    upper = jnp.concatenate([third, second], axis=0)
    keys = (left2_ref[:, :HD], upper[:, :HD])
    values = (left2_ref[:, HD:], upper[:, HD:])

    def write(rows, lanes, value):
        dq_ref[0, rows, lanes] = (value + near_ref[rows, lanes]).astype(BF)

    attend(q_rows, g_rows, keys, values, live_ref[1], acc_ref, lse_rows, delta_rows, write)
    low_ref[:C] = acc_ref[0, :C].astype(BF)
    low_ref[C:] = (acc_ref[0, C:] + jnp.where(last, acc_ref[1, :C], 0.0)).astype(BF)
    high_ref[...] = acc_ref[1].astype(BF)


def turn_kernel(count, idx_ref, kv_ref, high_ref, low2_ref, high2_ref, left_ref, right_ref):
    place = idx_ref[0]
    end, start = place >= count - 2, place < 2
    low2, high2 = low2_ref[:C].astype(F32), high2_ref[:C].astype(F32)
    mine = jnp.where(place == count - 1, high_ref[C:].astype(F32), 0.0)
    left_ref[:C] = (kv_ref[0, :C] + jnp.where(end, 0.0, low2) + mine).astype(BF)
    left_ref[C:] = jnp.where(end, low2, 0.0).astype(BF)
    right_ref[:C] = (kv_ref[1, :C] + jnp.where(start, 0.0, high2)).astype(BF)
    right_ref[C : 2 * C] = high_ref[C:]
    right_ref[2 * C :] = jnp.where(start, high2, 0.0).astype(BF)


def close_kernel(
    count,
    idx_ref,
    kv_ref,
    high_ref,
    low2_ref,
    high2_ref,
    right_ref,
    low1_ref,
    high1_ref,
    own_ref,
    cross_ref,
    spread_ref,
):
    place = idx_ref[0]
    last, before = place == count - 1, place == count - 2
    end, start = place >= count - 2, place < 2
    low2, high2 = low2_ref[C:].astype(F32), high2_ref[C:].astype(F32)
    low1, high1 = low1_ref[:C].astype(F32), high1_ref[:C].astype(F32)
    lower = kv_ref[0, C:] + jnp.where(end, 0.0, low2) + jnp.where(last, 0.0, low1)
    lower += jnp.where(last, high1_ref[C : 2 * C].astype(F32) + right_ref[:C].astype(F32), 0.0)
    lower += jnp.where(before, high_ref[:C].astype(F32), 0.0)
    upper = kv_ref[1, C:] + jnp.where(start, 0.0, high2) + jnp.where(place == 0, 0.0, high1)
    own_ref[:C] = lower
    own_ref[C:] = upper
    near_end = before | (place == count - 3)
    near_start = (place == 1) | (place == 2)
    back = jnp.where(end, low2, 0.0) + jnp.where(last, low1, 0.0)
    back += jnp.where(near_end, low1_ref[C:].astype(F32), 0.0)
    forth = jnp.where(start, high2, 0.0) + jnp.where(place == 0, high1, 0.0)
    forth += jnp.where(near_start, high1_ref[2 * C :].astype(F32), 0.0)
    cross = jnp.where(place >= count // 2, back, forth).astype(BF)
    cross_ref[...] = cross
    for i in range(spread_ref.shape[0]):
        spread_ref[i, :C] = lower[:, HD:].astype(BF)
        spread_ref[i, C : 2 * C] = upper[:, HD:].astype(BF)
        spread_ref[i, 2 * C :] = cross[:, HD:]


def finish_kernel(count, idx_ref, own_ref, cross_ref, dk_ref, dv_ref):
    first = idx_ref[0] < count // 2
    cross = cross_ref[...].astype(F32)
    lower = own_ref[:C] + jnp.where(first, cross, 0.0)
    upper = own_ref[C:] + jnp.where(first, 0.0, cross)
    dk_ref[0, :C] = lower[:, :HD].astype(BF)
    dk_ref[0, C:] = upper[:, :HD].astype(BF)
    dv_ref[0, :C] = lower[:, HD:].astype(BF)
    dv_ref[0, C:] = upper[:, HD:].astype(BF)


def chunk_kernel(tp_ref, x_ref, out_ref, sems):
    parts, _, width = out_ref.shape
    stride = x_ref.shape[2] // parts
    copies = []
    for i in range(parts):
        lanes = pl.ds(pl.multiple_of(i * stride + tp_ref[0] * width, 128), width)
        copies.append(pltpu.make_async_copy(x_ref.at[0, :, lanes], out_ref.at[i], sems.at[i]))
    for copy in copies:
        copy.start()
    for copy in copies:
        copy.wait()


def repeat_kernel(x_ref, out_ref):
    for i in range(out_ref.shape[0]):
        out_ref[i] = x_ref[...]


def weight_kernel(scale, core_ref, mine_ref, theirs_ref, dv_ref, out_ref):
    pieces, parts, tokens, width = mine_ref.shape
    each = out_ref.shape[0] // (2 * pieces)
    rows = []
    for i in range(parts):
        lower, upper = dv_ref[i, :C].astype(F32), dv_ref[i, C : 2 * C].astype(F32)
        cross = dv_ref[i ^ 1, 2 * C :].astype(F32)
        if i % 2 == 0:
            lower += cross
        else:
            upper += cross
        rows += [lower.astype(BF), upper.astype(BF)]
    dv = jnp.concatenate(rows, axis=0).T
    for i in range(pieces):
        for x_ref, core in ((mine_ref, core_ref[0]), (theirs_ref, 1 - core_ref[0])):
            x = x_ref[i].reshape(parts * tokens, width)
            flat = jnp.dot(dv, x, preferred_element_type=F32) * scale
            flat = flat.T.astype(BF).reshape(each, width // each, HD)
            out_ref[pl.ds((2 * i + core) * each, each)] = flat


def shift(value, by, wrap_half):
    length = lax.axis_size("ctx_1")
    pairs = [
        (h * length + z, h * length + (z + by) % length)
        for h in range(2)
        for z in range(length)
        if h == wrap_half or 0 <= z + by < length
    ]
    return lax.ppermute(value, CTX, pairs)


def swap(value, back):
    length = lax.axis_size("ctx_1")
    pairs = [(z, length + z) for z in range(length - 3, length)] + [(length + z, z) for z in range(3)]
    return lax.ppermute(value, CTX, [(b, a) for a, b in pairs] if back else pairs)


def body(layer_input, queries, key_heads, value_heads, attn_out, out_grad, log_sums, doc_ids):
    count = lax.axis_size(CTX)
    place = lax.axis_index(CTX).astype(jnp.int32).reshape(1)
    width = queries.shape[2]
    rows = 2 * C
    groups = lax.axis_size(ROWS)
    steps = lax.axis_size("ctx_1")
    pieces = lax.axis_size(TP)
    piece = layer_input.shape[2] // (groups * pieces)
    heads = width // HD
    group = min(4, heads)
    row_terms = shape((2, heads // group, group * C, 128), F32)
    head_rows = shape(row_terms.shape, BF)
    pair, block, three = (shape((n * C, 2 * HD), BF) for n in (2, 1, 3))
    at = functools.partial

    kv, cross = call(
        at(pack_kernel, count),
        [pair, block],
        [SMEM, ANY, ANY],
        1,
        [pltpu.VMEM((rows, HD), BF), pltpu.VMEM((rows, HD), BF), pltpu.SemaphoreType.DMA((2,))],
        mib=56,
    )(place, key_heads, value_heads)
    kv, part_of = lax.optimization_barrier((kv, lax.axis_index(TP).astype(jnp.int32).reshape(1)))
    cross = swap(cross, False)
    q_rows, g_rows, lse_rows, delta_rows, live = call(
        at(prepare_kernel, count),
        [head_rows, head_rows, row_terms, row_terms, shape((2, 2, C, 128), F32)],
        [SMEM] + [VMEM] * 5,
        COST["prepare"],
        mib=12,
    )(place, queries[0], out_grad[0], attn_out[0], log_sums[0], doc_ids)
    cross, live = lax.optimization_barrier((cross, live))
    (chunks,) = call(
        chunk_kernel,
        [shape((groups, rows, piece), BF)],
        [SMEM, ANY],
        2,
        [pltpu.SemaphoreType.DMA((groups,))],
    )(part_of, layer_input)
    mine = lax.all_to_all(chunks, ROWS, 0, 0, tiled=True)
    to_left, to_right = call(at(first_kernel, count), [pair, three], [SMEM] + [VMEM] * 2, COST["widen"])(
        place, kv, cross
    )
    left = shift(to_left, 1, 1)
    right = shift(to_right, -1, 0)
    low, high, send_low, send_high = call(
        at(widen_kernel, count), [pair] * 4, [SMEM] + [VMEM] * 4, COST["widen"]
    )(place, kv, cross, left, right)
    left2 = shift(send_low, 2, 1)
    right2 = shift(send_high, -2, 0)
    near_query, near_kv = call(
        near_kernel,
        [shape((rows, width), F32), shape((2, 128, 2 * HD), F32)],
        [SMEM] + [VMEM] * 7,
        COST["near"],
        mib=12,
    )(place, q_rows, g_rows, low, high, lse_rows, delta_rows, live)
    query_grad, far_low, far_high = call(
        at(far_kernel, count),
        [shape((1, rows, width), BF), pair, pair],
        [SMEM] + [VMEM] * 10,
        COST["far"],
        [pltpu.VMEM((2, 128, 2 * HD), F32)],
        mib=12,
    )(place, q_rows, g_rows, low, right, left2, right2, near_query, lse_rows, delta_rows, live)
    low2 = shift(far_low, -2, 1)
    high2 = shift(far_high, 2, 0)
    low2, mine = lax.optimization_barrier((low2, mine))
    (repeated,) = call(repeat_kernel, [shape((pieces // 2, groups, rows, piece), BF)], [VMEM], 1)(mine)
    tokens = lax.all_to_all(repeated, "tp_x", 0, 0, tiled=True)
    to_left, to_right = call(
        at(turn_kernel, count), [pair, three], [SMEM] + [VMEM] * 4, COST["turn"]
    )(place, near_kv, far_high, low2, high2)
    low1 = shift(to_left, -1, 1)
    high1 = shift(to_right, 1, 0)
    own, cross, spread = call(
        at(close_kernel, count),
        [shape((rows, 2 * HD), F32), block, shape((groups, 3 * C, HD), BF)],
        [SMEM] + [VMEM] * 7,
        COST["close"],
    )(place, near_kv, far_high, low2, high2, to_right, low1, high1)
    spread, tokens = lax.optimization_barrier((spread, tokens))
    tokens_2 = lax.ppermute(tokens, "core", [(0, 1), (1, 0)])
    everyone = lax.all_to_all(spread, ROWS, 0, 0, tiled=True)
    weight_scale = (lax.axis_size("dp") * doc_ids.shape[1]) ** (-0.5)
    (part,) = call(
        at(weight_kernel, weight_scale),
        [shape((steps, piece * pieces // steps, HD), BF)],
        [SMEM] + [VMEM] * 3,
        1,
        mib=12,
    )(lax.axis_index("core").astype(jnp.int32).reshape(1), tokens, tokens_2, everyone)
    part, cross = lax.optimization_barrier((part, cross))
    parts = lax.all_to_all(part, "ctx_1", 0, 0, tiled=True)
    cross = swap(cross, True)
    grad = shape((1, rows, HD), BF)
    key_grad, value_grad = call(at(finish_kernel, count), [grad, grad], [SMEM] + [VMEM] * 2, COST["finish"])(
        place, own, cross
    )
    weight_grad = jnp.sum(parts.astype(F32), axis=0)
    return (query_grad, key_grad, value_grad, weight_grad)


def solution(mesh):
    sizes = mesh.shape
    split = Mesh(
        mesh.devices.reshape(sizes["dp"], 2, sizes["ctx"] // 2, sizes["tp"] // 2, 2),
        ("dp", "ctx_0", "ctx_1", "tp_x", "core"),
    )
    in_specs = (
        P("dp", CTX, None),
        P("dp", CTX, TP),
        P("dp", CTX, TP),
        P("dp", CTX, TP),
        P("dp", CTX, TP),
        P("dp", CTX, TP),
        P("dp", TP, CTX),
        P("dp", None),
    )
    out_specs = (P("dp", CTX, TP), P("dp", CTX, TP), P("dp", CTX, TP), P(DP_CTX, TP))
    return jax.shard_map(body, mesh=split, in_specs=in_specs, out_specs=out_specs, check_vma=False)
```

```python
import functools

import jax
import jax.numpy as jnp
from jax import lax
from jax.experimental import pallas as pl
from jax.experimental.pallas import tpu as pltpu
from jax.sharding import Mesh
from jax.sharding import PartitionSpec as P

HD = 128
C = 64
CTX = ("ctx_0", "ctx_1")
ROWS = ("dp", "ctx_0")
DP_CTX = ("dp", "ctx_0", "ctx_1")
TP = ("tp_x", "core")
SCALE = HD ** (-0.5)
BF = jnp.bfloat16
F32 = jnp.float32
SMEM = pl.BlockSpec(memory_space=pltpu.SMEM)
VMEM = pl.BlockSpec(memory_space=pltpu.VMEM)
ANY = pl.BlockSpec(memory_space=pl.ANY)
COST = {"prepare": 4, "first": 4, "widen": 0.1, "repeat": 4, "near": 0.3, "far": 0.3, "turn": 10, "close": 5, "finish": 0.5}


def call(kernel, outs, in_specs, us, scratch=(), mib=8):
    return pl.pallas_call(
        kernel,
        name=getattr(kernel, "func", kernel).__name__,
        out_shape=outs,
        in_specs=in_specs,
        out_specs=[VMEM] * len(outs),
        scratch_shapes=list(scratch),
        compiler_params=pltpu.CompilerParams(vmem_limit_bytes=mib * 1024 * 1024),
        cost_estimate=pl.CostEstimate(flops=int(us * 1e9), bytes_accessed=0, transcendentals=0),
    )


def shape(dims, dtype):
    return jax.ShapeDtypeStruct(dims, dtype)


def doc_pair(doc_ref, block):
    first = jnp.maximum(block - 1, 0)
    chunk = first // 2
    ahead = jnp.minimum(chunk + 1, doc_ref.shape[1] // 128 - 1)
    here = doc_ref[:, pl.ds(pl.multiple_of(chunk * 128, 128), 128)]
    after = doc_ref[:, pl.ds(pl.multiple_of(ahead * 128, 128), 128)]
    lane = lax.broadcasted_iota(jnp.int32, (1, 128), 1)
    crossing = jnp.where(lane < C, pltpu.roll(here, C, 1), pltpu.roll(after, C, 1))
    start = jnp.where(block - 1 < 0, pltpu.roll(here, C, 1), here)
    return jnp.where(first % 2 == 0, start, crossing)


def live_pair(doc_ref, query_block, key_block):
    row = lax.broadcasted_iota(jnp.int32, (C, 128), 0)
    lane = lax.broadcasted_iota(jnp.int32, (C, 128), 1)
    own = doc_pair(doc_ref, query_block)
    query_doc = jnp.sum(jnp.where(lane == row + C, own, 0), axis=1, keepdims=True)
    key_doc = doc_pair(doc_ref, key_block)
    key_pos = (key_block - 1) * C + lane
    query_pos = query_block * C + row
    return (key_doc == query_doc) & (key_pos <= query_pos) & (key_pos >= 0)


def attend(q_rows, g_rows, keys, values, live, kv_acc, lse_rows, delta_rows, write_query):
    steps, group = q_rows.shape[1], q_rows.shape[2] // C

    def step(at, carry):
        lanes = pl.ds(pl.multiple_of(at * group * HD, group * HD), group * HD)
        for half in range(2):
            rows = slice(half * C, half * C + C)
            q, g = q_rows[half, at], g_rows[half, at]
            lse, delta = lse_rows[half, at], delta_rows[half, at]
            k, v = keys[half], values[half]
            dims = (((1,), (1,)), ((), ()))
            s = lax.dot_general(q, k, dims, preferred_element_type=F32)
            mask = jnp.concatenate([live[half]] * group, axis=0)
            p = jnp.where(mask > 0.0, jnp.exp(s * SCALE - lse), 0.0)
            dp = lax.dot_general(g, v, dims, preferred_element_type=F32)
            ds = (p * (dp - delta)).astype(BF)
            dq = jnp.dot(ds, k, preferred_element_type=F32) * SCALE
            tdims = (((0,), (0,)), ((), ()))
            dk = lax.dot_general(ds, q, tdims, preferred_element_type=F32) * SCALE
            dv = lax.dot_general(p.astype(BF), g, tdims, preferred_element_type=F32)
            kv_acc[half, :, :HD] += dk
            kv_acc[half, :, HD:] += dv
            wide = jnp.concatenate([dq[i * C : (i + 1) * C] for i in range(group)], axis=1)
            write_query(rows, lanes, wide)
        return carry

    kv_acc[...] = jnp.zeros_like(kv_acc)
    lax.fori_loop(0, steps, step, 0)


def pick(where, a, b):
    return jnp.where(where, a.astype(F32), b.astype(F32))


def pack_kernel(count, idx_ref, k_ref, v_ref, kv_ref, cross_ref, k_buf, v_buf, sems):
    copies = [
        pltpu.make_async_copy(k_ref.at[0], k_buf, sems.at[0]),
        pltpu.make_async_copy(v_ref.at[0], v_buf, sems.at[1]),
    ]
    for copy in copies:
        copy.start()
    for copy in copies:
        copy.wait()
    kv_ref[:, :HD] = k_buf[...]
    kv_ref[:, HD:] = v_buf[...]
    first = idx_ref[0] < count // 2
    cross_ref[:, :HD] = pick(first, k_buf[:C], k_buf[C:]).astype(BF)
    cross_ref[:, HD:] = pick(first, v_buf[:C], v_buf[C:]).astype(BF)


def first_kernel(count, idx_ref, kv_ref, cross_ref, left_ref, right_ref):
    place = idx_ref[0]
    left_ref[:C] = pick(place == count - 1, cross_ref[...], kv_ref[:C]).astype(BF)
    left_ref[C:] = cross_ref[...]
    right_ref[:C] = kv_ref[:C]
    right_ref[C : 2 * C] = pick(place == 0, cross_ref[...], kv_ref[C:]).astype(BF)
    right_ref[2 * C :] = cross_ref[...]


def widen_kernel(
    count, idx_ref, kv_ref, cross_ref, left_ref, right_ref, low_ref, high_ref, send_low_ref, send_high_ref
):
    place = idx_ref[0]
    lower, upper, other = kv_ref[:C], kv_ref[C:], cross_ref[...]
    before_lower = left_ref[:C]
    before_upper = pick(place == count - 1, lower, right_ref[C : 2 * C]).astype(BF)
    low_ref[:C] = before_lower
    low_ref[C:] = lower
    high_ref[:C] = before_upper
    high_ref[C:] = upper
    end, start = place >= count - 2, place < 2
    send_low_ref[:C] = pick(end, left_ref[C:], before_lower).astype(BF)
    send_low_ref[C:] = pick(end, other, lower).astype(BF)
    send_high_ref[:C] = pick(start, right_ref[2 * C :], before_upper).astype(BF)
    send_high_ref[C:] = pick(start, other, upper).astype(BF)


def prepare_kernel(
    count, idx_ref, q_ref, g_ref, o_ref, lse_ref, doc_ref, q_rows, g_rows, lse_rows, delta_rows, live_ref
):
    place = idx_ref[0]
    for half, block in enumerate((place, 2 * count - 1 - place)):
        live_ref[0, half] = live_pair(doc_ref, block, block).astype(F32)
        live_ref[1, half] = live_pair(doc_ref, block, block - 2).astype(F32)
    row = lax.broadcasted_iota(jnp.int32, (C, 128), 0)
    lane = lax.broadcasted_iota(jnp.int32, (C, 128), 1)
    group = lse_rows.shape[2] // C

    def step(at, carry):
        for half in range(2):
            rows = slice(half * C, half * C + C)
            for i in range(group):
                head = at * group + i
                lanes = pl.ds(pl.multiple_of(head * HD, HD), HD)
                g = g_ref[rows, lanes]
                delta = jnp.sum(g.astype(F32) * o_ref[rows, lanes].astype(F32), axis=1, keepdims=True)
                mine = jnp.where(lane == row + half * C, lse_ref[pl.ds(head, 1), :], 0.0)
                lse = jnp.sum(mine, axis=1, keepdims=True)
                into = slice(i * C, i * C + C)
                q_rows[half, at, into] = q_ref[rows, lanes]
                g_rows[half, at, into] = g
                delta_rows[half, at, into] = jnp.broadcast_to(delta, (C, 128))
                lse_rows[half, at, into] = jnp.broadcast_to(lse, (C, 128))
        return carry

    lax.fori_loop(0, lse_rows.shape[1], step, 0)


def near_kernel(idx_ref, q_rows, g_rows, low_ref, high_ref, lse_rows, delta_rows, live_ref, dq_ref, kv_ref):
    keys = (low_ref[:, :HD], high_ref[:, :HD])
    values = (low_ref[:, HD:], high_ref[:, HD:])

    def write(rows, lanes, value):
        dq_ref[rows, lanes] = value

    attend(q_rows, g_rows, keys, values, live_ref[0], kv_ref, lse_rows, delta_rows, write)


def far_kernel(
    count,
    idx_ref,
    q_rows,
    g_rows,
    near_low_ref,
    right_ref,
    left2_ref,
    right2_ref,
    near_ref,
    lse_rows,
    delta_rows,
    live_ref,
    dq_ref,
    low_ref,
    high_ref,
    acc_ref,
):
    place = idx_ref[0]
    last, before = place == count - 1, place == count - 2
    third = pick(before, near_low_ref[C:], pick(last, left2_ref[C:], right2_ref[:C])).astype(BF)
    second = pick(before, right_ref[:C], pick(last, near_low_ref[:C], right2_ref[C:])).astype(BF)
    upper = jnp.concatenate([third, second], axis=0)
    keys = (left2_ref[:, :HD], upper[:, :HD])
    values = (left2_ref[:, HD:], upper[:, HD:])

    def write(rows, lanes, value):
        dq_ref[0, rows, lanes] = (value + near_ref[rows, lanes]).astype(BF)

    attend(q_rows, g_rows, keys, values, live_ref[1], acc_ref, lse_rows, delta_rows, write)
    low_ref[:C] = acc_ref[0, :C].astype(BF)
    low_ref[C:] = (acc_ref[0, C:] + jnp.where(last, acc_ref[1, :C], 0.0)).astype(BF)
    high_ref[...] = acc_ref[1].astype(BF)


def turn_kernel(count, idx_ref, kv_ref, high_ref, low2_ref, high2_ref, left_ref, right_ref):
    place = idx_ref[0]
    end, start = place >= count - 2, place < 2
    low2, high2 = low2_ref[:C].astype(F32), high2_ref[:C].astype(F32)
    mine = jnp.where(place == count - 1, high_ref[C:].astype(F32), 0.0)
    left_ref[:C] = (kv_ref[0, :C] + jnp.where(end, 0.0, low2) + mine).astype(BF)
    left_ref[C:] = jnp.where(end, low2, 0.0).astype(BF)
    right_ref[:C] = (kv_ref[1, :C] + jnp.where(start, 0.0, high2)).astype(BF)
    right_ref[C : 2 * C] = high_ref[C:]
    right_ref[2 * C :] = jnp.where(start, high2, 0.0).astype(BF)


def close_kernel(
    count,
    idx_ref,
    kv_ref,
    high_ref,
    low2_ref,
    high2_ref,
    right_ref,
    low1_ref,
    high1_ref,
    own_ref,
    cross_ref,
    spread_ref,
):
    place = idx_ref[0]
    last, before = place == count - 1, place == count - 2
    end, start = place >= count - 2, place < 2
    low2, high2 = low2_ref[C:].astype(F32), high2_ref[C:].astype(F32)
    low1, high1 = low1_ref[:C].astype(F32), high1_ref[:C].astype(F32)
    lower = kv_ref[0, C:] + jnp.where(end, 0.0, low2) + jnp.where(last, 0.0, low1)
    lower += jnp.where(last, high1_ref[C : 2 * C].astype(F32) + right_ref[:C].astype(F32), 0.0)
    lower += jnp.where(before, high_ref[:C].astype(F32), 0.0)
    upper = kv_ref[1, C:] + jnp.where(start, 0.0, high2) + jnp.where(place == 0, 0.0, high1)
    own_ref[:C] = lower
    own_ref[C:] = upper
    near_end = before | (place == count - 3)
    near_start = (place == 1) | (place == 2)
    back = jnp.where(end, low2, 0.0) + jnp.where(last, low1, 0.0)
    back += jnp.where(near_end, low1_ref[C:].astype(F32), 0.0)
    forth = jnp.where(start, high2, 0.0) + jnp.where(place == 0, high1, 0.0)
    forth += jnp.where(near_start, high1_ref[2 * C :].astype(F32), 0.0)
    cross = jnp.where(place >= count // 2, back, forth).astype(BF)
    cross_ref[...] = cross
    for i in range(spread_ref.shape[0]):
        spread_ref[i, :C] = lower[:, HD:].astype(BF)
        spread_ref[i, C : 2 * C] = upper[:, HD:].astype(BF)
        spread_ref[i, 2 * C :] = cross[:, HD:]


def finish_kernel(count, idx_ref, own_ref, cross_ref, dk_ref, dv_ref):
    first = idx_ref[0] < count // 2
    cross = cross_ref[...].astype(F32)
    lower = own_ref[:C] + jnp.where(first, cross, 0.0)
    upper = own_ref[C:] + jnp.where(first, 0.0, cross)
    dk_ref[0, :C] = lower[:, :HD].astype(BF)
    dk_ref[0, C:] = upper[:, :HD].astype(BF)
    dv_ref[0, :C] = lower[:, HD:].astype(BF)
    dv_ref[0, C:] = upper[:, HD:].astype(BF)


def chunk_kernel(tp_ref, x_ref, out_ref, sems):
    parts, _, width = out_ref.shape
    stride = x_ref.shape[2] // parts
    copies = []
    for i in range(parts):
        lanes = pl.ds(pl.multiple_of(i * stride + tp_ref[0] * width, 128), width)
        copies.append(pltpu.make_async_copy(x_ref.at[0, :, lanes], out_ref.at[i], sems.at[i]))
    for copy in copies:
        copy.start()
    for copy in copies:
        copy.wait()


def repeat_kernel(mine_ref, theirs_ref, out_ref):
    for i in range(out_ref.shape[0]):
        out_ref[i, 0] = mine_ref[...]
        out_ref[i, 1] = theirs_ref[...]


def weight_kernel(scale, core_ref, x_ref, dv_ref, out_ref):
    pieces, _, parts, tokens, width = x_ref.shape
    each = out_ref.shape[0] // (2 * pieces)
    rows = []
    for i in range(parts):
        lower, upper = dv_ref[i, :C].astype(F32), dv_ref[i, C : 2 * C].astype(F32)
        cross = dv_ref[i ^ 1, 2 * C :].astype(F32)
        if i % 2 == 0:
            lower += cross
        else:
            upper += cross
        rows += [lower.astype(BF), upper.astype(BF)]
    dv = jnp.concatenate(rows, axis=0).T
    for i in range(pieces):
        for j, core in enumerate((core_ref[0], 1 - core_ref[0])):
            x = x_ref[i, j].reshape(parts * tokens, width)
            flat = jnp.dot(dv, x, preferred_element_type=F32) * scale
            flat = flat.T.astype(BF).reshape(each, width // each, HD)
            out_ref[pl.ds((2 * i + core) * each, each)] = flat


def shift(value, by, wrap_half):
    length = lax.axis_size("ctx_1")
    pairs = [
        (h * length + z, h * length + (z + by) % length)
        for h in range(2)
        for z in range(length)
        if h == wrap_half or 0 <= z + by < length
    ]
    return lax.ppermute(value, CTX, pairs)


def swap(value, back):
    length = lax.axis_size("ctx_1")
    pairs = [(z, length + z) for z in range(length - 3, length)] + [(length + z, z) for z in range(3)]
    return lax.ppermute(value, CTX, [(b, a) for a, b in pairs] if back else pairs)


def body(layer_input, queries, key_heads, value_heads, attn_out, out_grad, log_sums, doc_ids):
    count = lax.axis_size(CTX)
    place = lax.axis_index(CTX).astype(jnp.int32).reshape(1)
    width = queries.shape[2]
    rows = 2 * C
    groups = lax.axis_size(ROWS)
    steps = lax.axis_size("ctx_1")
    pieces = lax.axis_size(TP)
    piece = layer_input.shape[2] // (groups * pieces)
    heads = width // HD
    group = min(4, heads)
    row_terms = shape((2, heads // group, group * C, 128), F32)
    head_rows = shape(row_terms.shape, BF)
    pair, block, three = (shape((n * C, 2 * HD), BF) for n in (2, 1, 3))
    at = functools.partial

    kv, cross = call(
        at(pack_kernel, count),
        [pair, block],
        [SMEM, ANY, ANY],
        1,
        [pltpu.VMEM((rows, HD), BF), pltpu.VMEM((rows, HD), BF), pltpu.SemaphoreType.DMA((2,))],
        mib=56,
    )(place, key_heads, value_heads)
    kv, part_of = lax.optimization_barrier((kv, lax.axis_index(TP).astype(jnp.int32).reshape(1)))
    cross = swap(cross, False)
    (chunks,) = call(
        chunk_kernel,
        [shape((groups, rows, piece), BF)],
        [SMEM, ANY],
        2,
        [pltpu.SemaphoreType.DMA((groups,))],
    )(part_of, layer_input)
    mine = lax.all_to_all(chunks, ROWS, 0, 0, tiled=True)
    to_left, to_right = call(at(first_kernel, count), [pair, three], [SMEM] + [VMEM] * 2, COST["first"])(
        place, kv, cross
    )
    left = shift(to_left, 1, 1)
    right = shift(to_right, -1, 0)
    low, high, send_low, send_high = call(
        at(widen_kernel, count), [pair] * 4, [SMEM] + [VMEM] * 4, COST["widen"]
    )(place, kv, cross, left, right)
    _, mine = lax.optimization_barrier((send_low, mine))
    left2 = shift(send_low, 2, 1)
    right2 = shift(send_high, -2, 0)
    theirs = lax.ppermute(mine, "core", [(0, 1), (1, 0)])
    (repeated,) = call(
        repeat_kernel, [shape((pieces // 2, 2, groups, rows, piece), BF)], [VMEM] * 2, COST["repeat"]
    )(mine, theirs)
    tokens = lax.all_to_all(repeated, "tp_x", 0, 0, tiled=True)
    docs, repeated = lax.optimization_barrier((doc_ids, repeated))
    q_rows, g_rows, lse_rows, delta_rows, live = call(
        at(prepare_kernel, count),
        [head_rows, head_rows, row_terms, row_terms, shape((2, 2, C, 128), F32)],
        [SMEM] + [VMEM] * 5,
        COST["prepare"],
        mib=12,
    )(place, queries[0], out_grad[0], attn_out[0], log_sums[0], docs)
    near_query, near_kv = call(
        near_kernel,
        [shape((rows, width), F32), shape((2, 128, 2 * HD), F32)],
        [SMEM] + [VMEM] * 7,
        COST["near"],
        mib=12,
    )(place, q_rows, g_rows, low, high, lse_rows, delta_rows, live)
    query_grad, far_low, far_high = call(
        at(far_kernel, count),
        [shape((1, rows, width), BF), pair, pair],
        [SMEM] + [VMEM] * 10,
        COST["far"],
        [pltpu.VMEM((2, 128, 2 * HD), F32)],
        mib=12,
    )(place, q_rows, g_rows, low, right, left2, right2, near_query, lse_rows, delta_rows, live)
    low2 = shift(far_low, -2, 1)
    high2 = shift(far_high, 2, 0)
    to_left, to_right = call(
        at(turn_kernel, count), [pair, three], [SMEM] + [VMEM] * 4, COST["turn"]
    )(place, near_kv, far_high, low2, high2)
    low1 = shift(to_left, -1, 1)
    high1 = shift(to_right, 1, 0)
    own, cross, spread = call(
        at(close_kernel, count),
        [shape((rows, 2 * HD), F32), block, shape((groups, 3 * C, HD), BF)],
        [SMEM] + [VMEM] * 7,
        COST["close"],
    )(place, near_kv, far_high, low2, high2, to_right, low1, high1)
    spread, tokens = lax.optimization_barrier((spread, tokens))
    everyone = lax.all_to_all(spread, ROWS, 0, 0, tiled=True)
    weight_scale = (lax.axis_size("dp") * doc_ids.shape[1]) ** (-0.5)
    (part,) = call(
        at(weight_kernel, weight_scale),
        [shape((steps, piece * pieces // steps, HD), BF)],
        [SMEM] + [VMEM] * 2,
        1,
        mib=12,
    )(lax.axis_index("core").astype(jnp.int32).reshape(1), tokens, everyone)
    part, cross = lax.optimization_barrier((part, cross))
    parts = lax.all_to_all(part, "ctx_1", 0, 0, tiled=True)
    cross = swap(cross, True)
    grad = shape((1, rows, HD), BF)
    key_grad, value_grad = call(at(finish_kernel, count), [grad, grad], [SMEM] + [VMEM] * 2, COST["finish"])(
        place, own, cross
    )
    weight_grad = jnp.sum(parts.astype(F32), axis=0)
    return (query_grad, key_grad, value_grad, weight_grad)


def solution(mesh):
    sizes = mesh.shape
    split = Mesh(
        mesh.devices.reshape(sizes["dp"], 2, sizes["ctx"] // 2, sizes["tp"] // 2, 2),
        ("dp", "ctx_0", "ctx_1", "tp_x", "core"),
    )
    in_specs = (
        P("dp", CTX, None),
        P("dp", CTX, TP),
        P("dp", CTX, TP),
        P("dp", CTX, TP),
        P("dp", CTX, TP),
        P("dp", CTX, TP),
        P("dp", TP, CTX),
        P("dp", None),
    )
    out_specs = (P("dp", CTX, TP), P("dp", CTX, TP), P("dp", CTX, TP), P(DP_CTX, TP))
    return jax.shard_map(body, mesh=split, in_specs=in_specs, out_specs=out_specs, check_vma=False)
```

```python
import functools

import jax
import jax.numpy as jnp
from jax import lax
from jax.experimental import pallas as pl
from jax.experimental.pallas import tpu as pltpu
from jax.sharding import Mesh
from jax.sharding import PartitionSpec as P

HD = 128
C = 64
CTX = ("ctx_0", "ctx_1")
ROWS = ("dp", "ctx_0")
DP_CTX = ("dp", "ctx_0", "ctx_1")
TP = ("tp_x", "core")
SCALE = HD ** (-0.5)
BF = jnp.bfloat16
F32 = jnp.float32
SMEM = pl.BlockSpec(memory_space=pltpu.SMEM)
VMEM = pl.BlockSpec(memory_space=pltpu.VMEM)
ANY = pl.BlockSpec(memory_space=pl.ANY)
COST = {"prepare": 2, "first": 10, "widen": 0.1, "repeat": 1, "near": 0.3, "far": 0.3, "turn": 10, "close": 5, "finish": 0.5}


def call(kernel, outs, in_specs, us, scratch=(), mib=8):
    return pl.pallas_call(
        kernel,
        name=getattr(kernel, "func", kernel).__name__,
        out_shape=outs,
        in_specs=in_specs,
        out_specs=[VMEM] * len(outs),
        scratch_shapes=list(scratch),
        compiler_params=pltpu.CompilerParams(vmem_limit_bytes=mib * 1024 * 1024),
        cost_estimate=pl.CostEstimate(flops=int(us * 1e9), bytes_accessed=0, transcendentals=0),
    )


def shape(dims, dtype):
    return jax.ShapeDtypeStruct(dims, dtype)


def doc_pair(doc_ref, block):
    first = jnp.maximum(block - 1, 0)
    chunk = first // 2
    ahead = jnp.minimum(chunk + 1, doc_ref.shape[1] // 128 - 1)
    here = doc_ref[:, pl.ds(pl.multiple_of(chunk * 128, 128), 128)]
    after = doc_ref[:, pl.ds(pl.multiple_of(ahead * 128, 128), 128)]
    lane = lax.broadcasted_iota(jnp.int32, (1, 128), 1)
    crossing = jnp.where(lane < C, pltpu.roll(here, C, 1), pltpu.roll(after, C, 1))
    start = jnp.where(block - 1 < 0, pltpu.roll(here, C, 1), here)
    return jnp.where(first % 2 == 0, start, crossing)


def live_pair(doc_ref, query_block, key_block):
    row = lax.broadcasted_iota(jnp.int32, (C, 128), 0)
    lane = lax.broadcasted_iota(jnp.int32, (C, 128), 1)
    own = doc_pair(doc_ref, query_block)
    query_doc = jnp.sum(jnp.where(lane == row + C, own, 0), axis=1, keepdims=True)
    key_doc = doc_pair(doc_ref, key_block)
    key_pos = (key_block - 1) * C + lane
    query_pos = query_block * C + row
    return (key_doc == query_doc) & (key_pos <= query_pos) & (key_pos >= 0)


def attend(q_rows, g_rows, keys, values, live, kv_acc, lse_rows, delta_rows, write_query):
    steps, group = q_rows.shape[1], q_rows.shape[2] // C

    def step(at, carry):
        lanes = pl.ds(pl.multiple_of(at * group * HD, group * HD), group * HD)
        for half in range(2):
            rows = slice(half * C, half * C + C)
            q, g = q_rows[half, at], g_rows[half, at]
            lse, delta = lse_rows[half, at], delta_rows[half, at]
            k, v = keys[half], values[half]
            dims = (((1,), (1,)), ((), ()))
            s = lax.dot_general(q, k, dims, preferred_element_type=F32)
            mask = jnp.concatenate([live[half]] * group, axis=0)
            p = jnp.where(mask > 0.0, jnp.exp(s * SCALE - lse), 0.0)
            dp = lax.dot_general(g, v, dims, preferred_element_type=F32)
            ds = (p * (dp - delta)).astype(BF)
            dq = jnp.dot(ds, k, preferred_element_type=F32) * SCALE
            tdims = (((0,), (0,)), ((), ()))
            dk = lax.dot_general(ds, q, tdims, preferred_element_type=F32) * SCALE
            dv = lax.dot_general(p.astype(BF), g, tdims, preferred_element_type=F32)
            kv_acc[half, :, :HD] += dk
            kv_acc[half, :, HD:] += dv
            wide = jnp.concatenate([dq[i * C : (i + 1) * C] for i in range(group)], axis=1)
            write_query(rows, lanes, wide)
        return carry

    kv_acc[...] = jnp.zeros_like(kv_acc)
    lax.fori_loop(0, steps, step, 0)


def pick(where, a, b):
    return jnp.where(where, a.astype(F32), b.astype(F32))


def pack_kernel(count, idx_ref, k_ref, v_ref, kv_ref, cross_ref, k_buf, v_buf, sems):
    copies = [
        pltpu.make_async_copy(k_ref.at[0], k_buf, sems.at[0]),
        pltpu.make_async_copy(v_ref.at[0], v_buf, sems.at[1]),
    ]
    for copy in copies:
        copy.start()
    for copy in copies:
        copy.wait()
    kv_ref[:, :HD] = k_buf[...]
    kv_ref[:, HD:] = v_buf[...]
    first = idx_ref[0] < count // 2
    cross_ref[:, :HD] = pick(first, k_buf[:C], k_buf[C:]).astype(BF)
    cross_ref[:, HD:] = pick(first, v_buf[:C], v_buf[C:]).astype(BF)


def first_kernel(count, idx_ref, kv_ref, cross_ref, left_ref, right_ref):
    place = idx_ref[0]
    left_ref[:C] = pick(place == count - 1, cross_ref[...], kv_ref[:C]).astype(BF)
    left_ref[C:] = cross_ref[...]
    right_ref[:C] = kv_ref[:C]
    right_ref[C : 2 * C] = pick(place == 0, cross_ref[...], kv_ref[C:]).astype(BF)
    right_ref[2 * C :] = cross_ref[...]


def widen_kernel(
    count, idx_ref, kv_ref, cross_ref, left_ref, right_ref, low_ref, high_ref, send_low_ref, send_high_ref
):
    place = idx_ref[0]
    lower, upper, other = kv_ref[:C], kv_ref[C:], cross_ref[...]
    before_lower = left_ref[:C]
    before_upper = pick(place == count - 1, lower, right_ref[C : 2 * C]).astype(BF)
    low_ref[:C] = before_lower
    low_ref[C:] = lower
    high_ref[:C] = before_upper
    high_ref[C:] = upper
    end, start = place >= count - 2, place < 2
    send_low_ref[:C] = pick(end, left_ref[C:], before_lower).astype(BF)
    send_low_ref[C:] = pick(end, other, lower).astype(BF)
    send_high_ref[:C] = pick(start, right_ref[2 * C :], before_upper).astype(BF)
    send_high_ref[C:] = pick(start, other, upper).astype(BF)


def prepare_kernel(
    count, idx_ref, q_ref, g_ref, o_ref, lse_ref, doc_ref, q_rows, g_rows, lse_rows, delta_rows, live_ref
):
    place = idx_ref[0]
    for half, block in enumerate((place, 2 * count - 1 - place)):
        live_ref[0, half] = live_pair(doc_ref, block, block).astype(F32)
        live_ref[1, half] = live_pair(doc_ref, block, block - 2).astype(F32)
    row = lax.broadcasted_iota(jnp.int32, (C, 128), 0)
    lane = lax.broadcasted_iota(jnp.int32, (C, 128), 1)
    group = lse_rows.shape[2] // C

    def step(at, carry):
        for half in range(2):
            rows = slice(half * C, half * C + C)
            for i in range(group):
                head = at * group + i
                lanes = pl.ds(pl.multiple_of(head * HD, HD), HD)
                g = g_ref[rows, lanes]
                delta = jnp.sum(g.astype(F32) * o_ref[rows, lanes].astype(F32), axis=1, keepdims=True)
                mine = jnp.where(lane == row + half * C, lse_ref[pl.ds(head, 1), :], 0.0)
                lse = jnp.sum(mine, axis=1, keepdims=True)
                into = slice(i * C, i * C + C)
                q_rows[half, at, into] = q_ref[rows, lanes]
                g_rows[half, at, into] = g
                delta_rows[half, at, into] = jnp.broadcast_to(delta, (C, 128))
                lse_rows[half, at, into] = jnp.broadcast_to(lse, (C, 128))
        return carry

    lax.fori_loop(0, lse_rows.shape[1], step, 0)


def near_kernel(q_rows, g_rows, low_ref, high_ref, far_ref, lse_rows, delta_rows, live_ref, dq_ref, kv_ref):
    keys = (low_ref[:, :HD], high_ref[:, :HD])
    values = (low_ref[:, HD:], high_ref[:, HD:])

    def write(rows, lanes, value):
        dq_ref[0, rows, lanes] = (value + far_ref[rows, lanes]).astype(BF)

    attend(q_rows, g_rows, keys, values, live_ref[0], kv_ref, lse_rows, delta_rows, write)


def far_kernel(
    count,
    idx_ref,
    q_rows,
    g_rows,
    near_low_ref,
    right_ref,
    left2_ref,
    right2_ref,
    lse_rows,
    delta_rows,
    live_ref,
    dq_ref,
    low_ref,
    high_ref,
    acc_ref,
):
    place = idx_ref[0]
    last, before = place == count - 1, place == count - 2
    third = pick(before, near_low_ref[C:], pick(last, left2_ref[C:], right2_ref[:C])).astype(BF)
    second = pick(before, right_ref[:C], pick(last, near_low_ref[:C], right2_ref[C:])).astype(BF)
    upper = jnp.concatenate([third, second], axis=0)
    keys = (left2_ref[:, :HD], upper[:, :HD])
    values = (left2_ref[:, HD:], upper[:, HD:])

    def write(rows, lanes, value):
        dq_ref[rows, lanes] = value

    attend(q_rows, g_rows, keys, values, live_ref[1], acc_ref, lse_rows, delta_rows, write)
    low_ref[:C] = acc_ref[0, :C].astype(BF)
    low_ref[C:] = (acc_ref[0, C:] + jnp.where(last, acc_ref[1, :C], 0.0)).astype(BF)
    high_ref[...] = acc_ref[1].astype(BF)


def turn_kernel(count, idx_ref, kv_ref, high_ref, low2_ref, high2_ref, left_ref, right_ref):
    place = idx_ref[0]
    end, start = place >= count - 2, place < 2
    low2, high2 = low2_ref[:C].astype(F32), high2_ref[:C].astype(F32)
    mine = jnp.where(place == count - 1, high_ref[C:].astype(F32), 0.0)
    left_ref[:C] = (kv_ref[0, :C] + jnp.where(end, 0.0, low2) + mine).astype(BF)
    left_ref[C:] = jnp.where(end, low2, 0.0).astype(BF)
    right_ref[:C] = (kv_ref[1, :C] + jnp.where(start, 0.0, high2)).astype(BF)
    right_ref[C : 2 * C] = high_ref[C:]
    right_ref[2 * C :] = jnp.where(start, high2, 0.0).astype(BF)


def close_kernel(
    count,
    idx_ref,
    kv_ref,
    high_ref,
    low2_ref,
    high2_ref,
    right_ref,
    low1_ref,
    high1_ref,
    own_ref,
    cross_ref,
    spread_ref,
):
    place = idx_ref[0]
    last, before = place == count - 1, place == count - 2
    end, start = place >= count - 2, place < 2
    low2, high2 = low2_ref[C:].astype(F32), high2_ref[C:].astype(F32)
    low1, high1 = low1_ref[:C].astype(F32), high1_ref[:C].astype(F32)
    lower = kv_ref[0, C:] + jnp.where(end, 0.0, low2) + jnp.where(last, 0.0, low1)
    lower += jnp.where(last, high1_ref[C : 2 * C].astype(F32) + right_ref[:C].astype(F32), 0.0)
    lower += jnp.where(before, high_ref[:C].astype(F32), 0.0)
    upper = kv_ref[1, C:] + jnp.where(start, 0.0, high2) + jnp.where(place == 0, 0.0, high1)
    own_ref[:C] = lower
    own_ref[C:] = upper
    near_end = before | (place == count - 3)
    near_start = (place == 1) | (place == 2)
    back = jnp.where(end, low2, 0.0) + jnp.where(last, low1, 0.0)
    back += jnp.where(near_end, low1_ref[C:].astype(F32), 0.0)
    forth = jnp.where(start, high2, 0.0) + jnp.where(place == 0, high1, 0.0)
    forth += jnp.where(near_start, high1_ref[2 * C :].astype(F32), 0.0)
    cross = jnp.where(place >= count // 2, back, forth).astype(BF)
    cross_ref[...] = cross
    for i in range(spread_ref.shape[0]):
        spread_ref[i, :C] = lower[:, HD:].astype(BF)
        spread_ref[i, C : 2 * C] = upper[:, HD:].astype(BF)
        spread_ref[i, 2 * C :] = cross[:, HD:]


def finish_kernel(count, idx_ref, own_ref, cross_ref, dk_ref, dv_ref):
    first = idx_ref[0] < count // 2
    cross = cross_ref[...].astype(F32)
    lower = own_ref[:C] + jnp.where(first, cross, 0.0)
    upper = own_ref[C:] + jnp.where(first, 0.0, cross)
    dk_ref[0, :C] = lower[:, :HD].astype(BF)
    dk_ref[0, C:] = upper[:, :HD].astype(BF)
    dv_ref[0, :C] = lower[:, HD:].astype(BF)
    dv_ref[0, C:] = upper[:, HD:].astype(BF)


def chunk_kernel(tp_ref, x_ref, out_ref, sems):
    parts, _, width = out_ref.shape
    stride = x_ref.shape[2] // parts
    copies = []
    for i in range(parts):
        lanes = pl.ds(pl.multiple_of(i * stride + tp_ref[0] * width, 128), width)
        copies.append(pltpu.make_async_copy(x_ref.at[0, :, lanes], out_ref.at[i], sems.at[i]))
    for copy in copies:
        copy.start()
    for copy in copies:
        copy.wait()


def repeat_kernel(x_ref, out_ref):
    for i in range(out_ref.shape[0]):
        out_ref[i] = x_ref[...]


def weight_kernel(scale, x_ref, dv_ref, out_ref):
    pieces, parts, tokens, width = x_ref.shape
    each = out_ref.shape[0] // pieces
    rows = []
    for i in range(parts):
        lower, upper = dv_ref[i, :C].astype(F32), dv_ref[i, C : 2 * C].astype(F32)
        cross = dv_ref[i ^ 1, 2 * C :].astype(F32)
        if i % 2 == 0:
            lower += cross
        else:
            upper += cross
        rows += [lower.astype(BF), upper.astype(BF)]
    dv = jnp.concatenate(rows, axis=0).T
    for i in range(pieces):
        x = x_ref[i].reshape(parts * tokens, width)
        flat = jnp.dot(dv, x, preferred_element_type=F32) * scale
        out_ref[i * each : (i + 1) * each] = flat.T.astype(BF).reshape(each, width // each, HD)


def shift(value, by, wrap_half):
    length = lax.axis_size("ctx_1")
    pairs = [
        (h * length + z, h * length + (z + by) % length)
        for h in range(2)
        for z in range(length)
        if h == wrap_half or 0 <= z + by < length
    ]
    return lax.ppermute(value, CTX, pairs)


def swap(value, back):
    length = lax.axis_size("ctx_1")
    pairs = [(z, length + z) for z in range(length - 3, length)] + [(length + z, z) for z in range(3)]
    return lax.ppermute(value, CTX, [(b, a) for a, b in pairs] if back else pairs)


def body(layer_input, queries, key_heads, value_heads, attn_out, out_grad, log_sums, doc_ids):
    count = lax.axis_size(CTX)
    place = lax.axis_index(CTX).astype(jnp.int32).reshape(1)
    width = queries.shape[2]
    rows = 2 * C
    groups = lax.axis_size(ROWS)
    steps = lax.axis_size("ctx_1")
    pieces = lax.axis_size("tp_x")
    piece = layer_input.shape[2] // (groups * pieces)
    heads = width // HD
    group = min(4, heads)
    row_terms = shape((2, heads // group, group * C, 128), F32)
    head_rows = shape(row_terms.shape, BF)
    pair, block, three = (shape((n * C, 2 * HD), BF) for n in (2, 1, 3))
    at = functools.partial

    kv, cross = call(
        at(pack_kernel, count),
        [pair, block],
        [SMEM, ANY, ANY],
        1,
        [pltpu.VMEM((rows, HD), BF), pltpu.VMEM((rows, HD), BF), pltpu.SemaphoreType.DMA((2,))],
        mib=56,
    )(place, key_heads, value_heads)
    kv, part_of = lax.optimization_barrier((kv, lax.axis_index("tp_x").astype(jnp.int32).reshape(1)))
    cross = swap(cross, False)
    (chunks,) = call(
        chunk_kernel,
        [shape((groups, rows, piece), BF)],
        [SMEM, ANY],
        2,
        [pltpu.SemaphoreType.DMA((groups,))],
    )(part_of, layer_input)
    mine = lax.all_to_all(chunks, ROWS, 0, 0, tiled=True)
    to_left, to_right = call(at(first_kernel, count), [pair, three], [SMEM] + [VMEM] * 2, COST["first"])(
        place, kv, cross
    )
    left = shift(to_left, 1, 1)
    right = shift(to_right, -1, 0)
    low, high, send_low, send_high = call(
        at(widen_kernel, count), [pair] * 4, [SMEM] + [VMEM] * 4, COST["widen"]
    )(place, kv, cross, left, right)
    left2 = shift(send_low, 2, 1)
    right2 = shift(send_high, -2, 0)
    left2, mine = lax.optimization_barrier((left2, mine))
    (repeated,) = call(
        repeat_kernel, [shape((pieces, groups, rows, piece), BF)], [VMEM], COST["repeat"]
    )(mine)
    tokens = lax.all_to_all(repeated, "tp_x", 0, 0, tiled=True)
    docs, repeated = lax.optimization_barrier((doc_ids, repeated))
    q_rows, g_rows, lse_rows, delta_rows, live = call(
        at(prepare_kernel, count),
        [head_rows, head_rows, row_terms, row_terms, shape((2, 2, C, 128), F32)],
        [SMEM] + [VMEM] * 5,
        COST["prepare"],
        mib=12,
    )(place, queries[0], out_grad[0], attn_out[0], log_sums[0], docs)
    far_query, far_low, far_high = call(
        at(far_kernel, count),
        [shape((rows, width), F32), pair, pair],
        [SMEM] + [VMEM] * 9,
        COST["far"],
        [pltpu.VMEM((2, 128, 2 * HD), F32)],
        mib=12,
    )(place, q_rows, g_rows, low, right, left2, right2, lse_rows, delta_rows, live)
    low2 = shift(far_low, -2, 1)
    high2 = shift(far_high, 2, 0)
    query_grad, near_kv = call(
        near_kernel,
        [shape((1, rows, width), BF), shape((2, 128, 2 * HD), F32)],
        [VMEM] * 8,
        COST["near"],
        mib=12,
    )(q_rows, g_rows, low, high, far_query, lse_rows, delta_rows, live)
    to_left, to_right = call(
        at(turn_kernel, count), [pair, three], [SMEM] + [VMEM] * 4, COST["turn"]
    )(place, near_kv, far_high, low2, high2)
    low1 = shift(to_left, -1, 1)
    high1 = shift(to_right, 1, 0)
    own, cross, spread = call(
        at(close_kernel, count),
        [shape((rows, 2 * HD), F32), block, shape((groups, 3 * C, HD), BF)],
        [SMEM] + [VMEM] * 7,
        COST["close"],
    )(place, near_kv, far_high, low2, high2, to_right, low1, high1)
    spread, tokens = lax.optimization_barrier((spread, tokens))
    everyone = lax.all_to_all(spread, ROWS, 0, 0, tiled=True)
    weight_scale = (lax.axis_size("dp") * doc_ids.shape[1]) ** (-0.5)
    (part,) = call(
        at(weight_kernel, weight_scale),
        [shape((steps, piece * pieces // steps, HD), BF)],
        [VMEM] * 2,
        1,
        mib=12,
    )(tokens, everyone)
    part, cross = lax.optimization_barrier((part, cross))
    parts = lax.all_to_all(part, "ctx_1", 0, 0, tiled=True)
    cross = swap(cross, True)
    grad = shape((1, rows, HD), BF)
    key_grad, value_grad = call(at(finish_kernel, count), [grad, grad], [SMEM] + [VMEM] * 2, COST["finish"])(
        place, own, cross
    )
    weight_grad = jnp.sum(parts.astype(F32), axis=0)
    return (query_grad, key_grad, value_grad, weight_grad)


def solution(mesh):
    sizes = mesh.shape
    split = Mesh(
        mesh.devices.reshape(sizes["dp"], 2, sizes["ctx"] // 2, sizes["tp"] // 2, 2),
        ("dp", "ctx_0", "ctx_1", "tp_x", "core"),
    )
    in_specs = (
        P("dp", CTX, None),
        P("dp", CTX, TP),
        P("dp", CTX, TP),
        P("dp", CTX, TP),
        P("dp", CTX, TP),
        P("dp", CTX, TP),
        P("dp", TP, CTX),
        P("dp", None),
    )
    out_specs = (P("dp", CTX, TP), P("dp", CTX, TP), P("dp", CTX, TP), P(DP_CTX, TP))
    return jax.shard_map(body, mesh=split, in_specs=in_specs, out_specs=out_specs, check_vma=False)
```
